32 devices in a mesh: groups: 2 (over x), orb: 16 (over z, y, core).
Axes of the slice: x: 2, y: 2, z: 4, core: 2. Of those that a mesh axis runs over, the one named last changes fastest.
Arguments:
- phi: bfloat16 [512, 32768], P(('groups', 'orb')), parts along dimension 0, may hold values from -6 to 6
- offsets: int32 [512, 3], P('groups'), parts along dimension 0, may hold values from 0 to 1
- fetch: int32 [32, 16], P(('groups', 'orb')), parts along dimension 0, may hold values from -1 to 15, as said below
- task_pairs: int32 [1536, 2], P(('groups', 'orb')), parts along dimension 0, may hold values from 0 to 15, as said below
- task_count: int32 [32], P(('groups', 'orb')), parts along dimension 0, may hold values from 6 to 48, as said below
Outputs:
- exchange_potential: float32 [512, 32768], P(('groups', 'orb')), parts along dimension 0
The draws below stay inside these ranges and needn't reach their ends.
There are 2 independent parts, one for each index of `groups`. The reference program is written for one: setup_inputs(seed, part) draws one part's arguments, and reference() takes and returns one part's arrays. A program takes and returns all parts, laid end to end along the dimension named above; each array names one. Nothing has to cross between parts.
Inputs may be any that keep to these rules, and one draw needn't show every extreme that they name: `fetch`: -1 means nothing is requested; device d requests 16 - 1 from itself, something from owner d + 1 (cyclic), and something from at least half of the owners. `task_pairs`: every owner named in a slot of a device has a request other than -1 in that device's fetch row; no owner is the first owner of more than 6 of one device's slots, and each device is the first owner of exactly 6 of its own slots. `task_count`: each count is 48 divided by 1, 2, 4 or 8.
All inputs are finite; a program needn't handle non-finite values.
Results may differ from the reference program's by a relative error of at most 0.0003.
Values may be sent and summed in bfloat16 or wider, within the bound.
No kernel may reach another device: no remote copies, remote signals or barrier semaphores. Data moves between devices by JAX's collectives and lax.ppermute only.
A program may use at most 128 MiB of HBM per device.

```python
import jax
import jax.numpy as jnp
from jax import lax

P_SIZE = 32
ORB_DEV = 16
TASK_DEV = 48
ORBS = 256
CAP = 6
N_ORB = 16


def plan_rows(key):
    score_key = jax.random.fold_in(key, 11)
    local_key = jax.random.fold_in(key, 12)
    keep_key = jax.random.fold_in(key, 15)
    counter = jnp.arange(N_ORB)
    distance = (counter[None, :] - counter[:, None]) % N_ORB
    raw_scores = jax.random.randint(score_key, (N_ORB, N_ORB), 0, N_ORB)
    scores = raw_scores * N_ORB + distance
    scores = jnp.where(distance == 0, -2, jnp.where(distance == 1, -1, scores))
    ordering = jnp.argsort(scores, axis=1).astype(jnp.int32)
    ranking = jnp.argsort(ordering, axis=1).astype(jnp.int32)
    keeping = jax.random.randint(keep_key, (N_ORB, 1), N_ORB // 2, N_ORB)
    local = jax.random.randint(local_key, (N_ORB, N_ORB), 0, ORB_DEV)
    result = jnp.where(ranking < keeping, local, -1)
    result = jnp.where(distance == 0, ORB_DEV - 1, result)
    return (result.astype(jnp.int32), ordering)


def draw_fetch(key, part):
    result, ordering = plan_rows(key)
    return result


def draw_task_pairs(key, part):
    requests, ordering = plan_rows(key)
    tickets = N_ORB // 2 * CAP
    remaining = tickets - CAP - 1
    pick_keys = jax.random.split(jax.random.fold_in(key, 16), N_ORB)
    picks = jax.vmap(lambda one_key: jax.random.permutation(one_key, remaining))(pick_keys)
    picks = picks[:, :TASK_DEV - CAP - 1] + CAP + 1
    fixed_part = jnp.broadcast_to(jnp.arange(CAP)[None, :], (N_ORB, CAP))
    rest = jnp.concatenate([fixed_part.astype(jnp.int32), picks.astype(jnp.int32)], axis=1)
    shuffle_keys = jax.random.split(jax.random.fold_in(key, 17), N_ORB)
    rest = jax.vmap(lambda one_key, row: jax.random.permutation(one_key, row))(shuffle_keys, rest)
    leading = jnp.full((N_ORB, 1), CAP, jnp.int32)
    chosen = jnp.concatenate([leading, rest.astype(jnp.int32)], axis=1)
    first_owner = jnp.take_along_axis(ordering, (chosen // CAP).astype(jnp.int32), axis=1)
    pair_key = jax.random.fold_in(key, 13)
    raw_second = jax.random.randint(pair_key, (N_ORB, TASK_DEV), 0, N_ORB)
    following = ((jnp.arange(N_ORB) + 1) % N_ORB).astype(jnp.int32)
    raw_second = raw_second.at[:, 0].set(following)
    valid = jnp.take_along_axis(requests, raw_second, axis=1) >= 0
    own_slot = jnp.broadcast_to(jnp.arange(N_ORB)[:, None], raw_second.shape)
    second_owner = jnp.where(valid, raw_second, own_slot)
    paired = jnp.stack([first_owner, second_owner], axis=2)
    return paired.reshape(N_ORB * TASK_DEV, 2).astype(jnp.int32)


def draw_task_count(key, part):
    count_key = jax.random.fold_in(key, 14)
    powers = jax.random.randint(count_key, (N_ORB,), 0, 4)
    counts = TASK_DEV // jnp.left_shift(jnp.ones((N_ORB,), jnp.int32), powers)
    counts = counts.at[0].set(TASK_DEV)
    counts = counts.at[1].set(TASK_DEV // 8)
    return counts.astype(jnp.int32)


def with_ends(values, key, least, largest):
    longest = values.shape.index(max(values.shape))
    spots = []
    for shift in (0, 1):
        where = [jax.random.randint(jax.random.fold_in(key, axis), (), 0, length) for axis, length in enumerate(values.shape)]
        where[longest] = (where[longest] + shift) % values.shape[longest]
        spots.append(tuple(where))
    return values.at[spots[0]].set(least).at[spots[1]].set(largest)


def block_levels(stream_key, shape, shards, low, top_value):
    def one(axis_at, blocks):
        draws = jax.random.uniform(jax.random.fold_in(jax.random.fold_in(stream_key, 6), axis_at), (blocks,), jnp.float32, low / len(shards), top_value / len(shards))
        return jnp.repeat(jnp.exp(draws), shape[axis_at] // blocks).reshape((-1,) + (1,) * (len(shape) - axis_at - 1))

    gain = one(*shards[0])
    for cut in shards[1:]:
        gain = gain * one(*cut)
    return gain


def noise(own_key, dims, scale, limit, cuts=(), kind=jnp.bfloat16):
    factor_of = block_levels(own_key, dims, cuts, -0.22, 0.18) if cuts else 1.0
    values = jax.random.normal(own_key, dims, jnp.float32) * scale * factor_of
    return jnp.minimum(jnp.maximum(values, -limit), limit).astype(kind)


def setup_inputs(seed: int = 0, part: int = 0) -> dict:
    keys = jax.random.split(jax.random.key(seed), 6)
    part_keys = jax.random.split(jax.random.fold_in(keys[5], part), 6)
    phi = noise(part_keys[0], (ORBS, P_SIZE ** 3), 1.0, 6.0, ((0, 16),))
    offsets = with_ends(jax.random.randint(part_keys[1], (ORBS, 3), 0, 2), jax.random.fold_in(part_keys[1], 1), 0, 1).astype(jnp.int32)
    fetch = draw_fetch(jax.random.fold_in(jax.random.fold_in(keys[5], part), 71), part)
    task_pairs = draw_task_pairs(jax.random.fold_in(jax.random.fold_in(keys[5], part), 71), part)
    task_count = draw_task_count(jax.random.fold_in(jax.random.fold_in(keys[5], part), 71), part)
    return {"phi": phi, "offsets": offsets, "fetch": fetch, "task_pairs": task_pairs, "task_count": task_count}


task_batch = 8

def sine_table(length):
    counter = jnp.arange(length).astype(jnp.float32) + 1.0
    return jnp.sqrt(2.0 / (length + 1)) * jnp.sin(jnp.pi * counter[:, None] * counter[None, :] / (length + 1))

def inverse_eigen(length):
    counter = jnp.arange(length).astype(jnp.float32) + 1.0
    eigen = 2.0 - 2.0 * jnp.cos(jnp.pi * counter / (length + 1))
    total = eigen[:, None, None] + eigen[None, :, None] + eigen[None, None, :]
    return (1.0 / total).reshape(length, length * length)

def solve_box(density, table_x, table_yz, inverse):
    highest = lax.Precision.HIGHEST
    spectrum = jnp.einsum('kx,bxm->bkm', table_x, density, precision=highest)
    spectrum = jnp.einsum('bkm,nm->bkn', spectrum, table_yz, precision=highest)
    spectrum = spectrum * inverse[None]
    potential = jnp.einsum('kx,bxm->bkm', table_x, spectrum, precision=highest)
    return jnp.einsum('bkm,nm->bkn', potential, table_yz, precision=highest)

def move_flat(patch_flat, offset_diff, length):
    half_cells = length // 2
    volume = length * length * length
    margin = half_cells * (length * length + length + 1)
    places = jnp.arange(volume).astype(jnp.int32)
    coord_x = places // (length * length)
    coord_y = places // length % length
    coord_z = places % length
    step_x = coord_x + half_cells * offset_diff[0]
    step_y = coord_y + half_cells * offset_diff[1]
    step_z = coord_z + half_cells * offset_diff[2]
    inside = (step_x >= 0) & (step_x < length) & (step_y >= 0) & (step_y < length) & (step_z >= 0) & (step_z < length)
    shift_flat = half_cells * (offset_diff[0] * length * length + offset_diff[1] * length + offset_diff[2])
    padded = jnp.pad(patch_flat, margin)
    start = (margin + shift_flat).astype(jnp.int32)
    moved = lax.dynamic_slice(padded, (start,), (volume,))
    return jnp.where(inside, moved, jnp.zeros_like(moved))

def pair_terms(first_patch, second_patch, offset_diff, live, length):
    count = first_patch.shape[0]
    table_x = sine_table(length)
    table_yz = jnp.kron(table_x, table_x)
    inverse = inverse_eigen(length)
    moved = jax.vmap(lambda patch_flat, diff: move_flat(patch_flat, diff, length))(second_patch, offset_diff.astype(jnp.int32))
    moved = moved.reshape(count, length, length * length).astype(jnp.float32)
    density = first_patch.reshape(count, length, length * length).astype(jnp.float32) * moved
    potential = solve_box(density, table_x, table_yz, inverse)
    return (potential * moved * live[:, None, None]).reshape(count, length ** 3)

def reference(phi, offsets, fetch, task_pairs, task_count):
    slots = task_pairs.reshape(N_ORB, TASK_DEV, 2)
    first_ids = slots[:, :, 0] * ORB_DEV + jnp.take_along_axis(fetch, slots[:, :, 0], axis=1)
    second_ids = slots[:, :, 1] * ORB_DEV + jnp.take_along_axis(fetch, slots[:, :, 1], axis=1)
    live = (jnp.arange(TASK_DEV)[None, :] < task_count[:, None]).astype(jnp.float32)
    first_ids = first_ids.astype(jnp.int32).reshape(-1, task_batch)
    second_ids = second_ids.astype(jnp.int32).reshape(-1, task_batch)
    live = live.reshape(-1, task_batch)

    def run_block(totals, pieces):
        first_block, second_block, live_block = pieces
        offset_diff = offsets[first_block] - offsets[second_block]
        terms = pair_terms(phi[first_block], phi[second_block], offset_diff, live_block, P_SIZE)
        return (totals.at[first_block].add(terms), None)
    start_totals = jnp.zeros((ORBS, P_SIZE ** 3), jnp.float32)
    totals, unused = lax.scan(run_block, start_totals, (first_ids, second_ids, live))
    return totals
```

```python
import functools

import jax
import jax.numpy as jnp
import ml_dtypes
import numpy as np
from jax import lax
from jax.experimental import pallas as pl
from jax.experimental.pallas import tpu as pltpu
from jax.sharding import PartitionSpec as P

BLOCK = 8
LEVELS = 32704.0
BF16 = jnp.bfloat16
F32 = jnp.float32


def cube_root(volume):
    length = 1
    while length * length * length < volume:
        length = length + 1
    return length


def split_bf16(values):
    high = values.astype(ml_dtypes.bfloat16)
    low = (values - high.astype(np.float64)).astype(ml_dtypes.bfloat16)
    return high, low


def host_tables(length):
    half = length // 2
    area = half * half
    count = np.arange(length) + 1.0
    sine = np.sqrt(2.0 / (length + 1)) * np.sin(np.pi * np.outer(count, count) / (length + 1))
    eigen = 2.0 - 2.0 * np.cos(np.pi * count / (length + 1))
    fold = [sine[parity::2, :half].T for parity in (0, 1)]
    forward, backward, factors = [], [], []
    for par_y in (0, 1):
        for par_z in (0, 1):
            table = np.kron(fold[par_y], fold[par_z])
            high, low = split_bf16(table)
            forward.append(np.concatenate([high, high, low], axis=0))
            high, low = split_bf16(table.T)
            backward.append(np.concatenate([high, high, low], axis=0))
            beta = 2.0 + (eigen[par_y::2][:, None] + eigen[par_z::2][None, :]).reshape(area)
            rows = [1.0 / beta]
            for _ in range(length - 1):
                rows.append(1.0 / (beta - rows[-1]))
            rows = np.stack(rows).astype(np.float32)
            factors.append(rows[:, : area // 2])
            factors.append(rows[:, area // 2 :])
    place = np.arange(area)
    low_y, low_z = place // half, place % half
    variants = []
    for rev_y, rev_z in ((0, 1), (1, 0), (1, 1)):
        src_y = half - 1 - low_y if rev_y else low_y
        src_z = half - 1 - low_z if rev_z else low_z
        one_hot = np.zeros((area, area), ml_dtypes.bfloat16)
        one_hot[src_y * half + src_z, place] = 1
        variants.append(one_hot)
    wide = 2 * area
    spot = np.arange(wide)
    pack = np.zeros((wide, wide), ml_dtypes.bfloat16)
    z_half, rest = spot // area, spot % area
    pack[(rest // half) * length + z_half * half + rest % half, spot] = 1
    unpack = []
    for par_y in (0, 1):
        y_nat = half - 1 - rest // half if par_y else rest // half
        z_nat = np.where(z_half == 1, length - 1 - rest % half, rest % half)
        one_hot = np.zeros((wide, wide), ml_dtypes.bfloat16)
        one_hot[spot, y_nat * length + z_nat] = 1
        unpack.append(one_hot)
    return dict(
        forward=np.stack(forward),
        backward=np.stack(backward),
        factors=np.stack(factors),
        variants=np.concatenate(variants, axis=1),
        pack=pack,
        unpack=np.stack(unpack),
    )


def halves(value):
    high = value.astype(BF16)
    low = (value - high.astype(F32)).astype(BF16)
    return high, low


def pack_kernel(phi_ref, table_ref, out_ref, work):
    orbs = phi_ref.shape[0]
    length = out_ref.shape[1]
    plane = length * length
    wide = plane // 2
    for y_half in range(2):
        rows = jnp.concatenate(
            [phi_ref[:, x * plane + y_half * wide : x * plane + (y_half + 1) * wide] for x in range(length)],
            axis=0,
        )
        moved = jnp.dot(rows, table_ref[...], preferred_element_type=F32)
        for j in range(wide // 128):
            work[y_half * (wide // 128) + j] = moved[:, j * 128 : (j + 1) * 128]
    for orb in range(orbs):
        for j in range(plane // 128):
            piece = work[j, pl.ds(orb, length, stride=orbs), :]
            out_ref[orb, :, j * 128 : (j + 1) * 128] = piece.astype(BF16)


def solve_kernel(
    orbs, fetch_ref, offsets_ref, pairs_ref, count_ref, in_ref, fwd_ref, bwd_ref, fac_ref, var_ref,
    out_ref, octs, grid_work, totals,
):
    nodes, length = in_ref.shape[0], in_ref.shape[1]
    half = length // 2
    area = half * half
    zero_at = nodes * 32
    octs[zero_at] = jnp.zeros((half, area), BF16)
    group = 8

    def make_variants(step, carry):
        for quad in range(4):
            block = in_ref[pl.ds(step * group, group), :, quad * area : (quad + 1) * area]
            turned = jnp.dot(
                block.reshape(group * length, area), var_ref[...], preferred_element_type=F32
            ).astype(BF16)
            for one in range(group):
                for hx in range(2):
                    base = (((step * group + one) * 2 + hx) * 4 + quad) * 4
                    octs[base] = block[one, hx * half : (hx + 1) * half]
                    first = one * length + hx * half
                    for rev in range(3):
                        octs[base + 1 + rev] = turned[first : first + half, rev * area : (rev + 1) * area]
        return carry

    lax.fori_loop(0, nodes // group, make_variants, 0)

    def clear(step, carry):
        totals[step] = jnp.zeros((half, area), F32)
        return carry

    lax.fori_loop(0, nodes * 8, clear, 0)
    live_count = count_ref[0]
    last_slot = pairs_ref.shape[0] // 2 - 1

    def task(slot):
        at = jnp.minimum(slot, last_slot)
        first, second = pairs_ref[2 * at], pairs_ref[2 * at + 1]
        id_a = first * orbs + jnp.maximum(fetch_ref[first], 0)
        id_b = second * orbs + jnp.maximum(fetch_ref[second], 0)
        diff = [offsets_ref[id_a * 3 + k] - offsets_ref[id_b * 3 + k] for k in range(3)]
        return first, second, diff, slot < live_count

    def second_at(second, diff, live, hx, py, pz):
        sx, sy, sz = hx + diff[0], py + diff[1], pz + diff[2]
        inside = live & (sx >= 0) & (sx < 2) & (sy >= 0) & (sy < 2) & (sz >= 0) & (sz < 2)
        found = (((second * 2 + sx) * 2 + sy) * 2 + sz) * 4 + (py * 2 + pz)
        return jnp.where(inside, found, zero_at)

    def run_block(step, carry):
        places = []
        for t in range(BLOCK):
            first, second, diff, live = task(step * BLOCK + t)
            spots = [
                [second_at(second, diff, live, hx, py, pz) for py in range(2) for pz in range(2)]
                for hx in range(2)
            ]
            places.append((first, spots))
        for t in range(BLOCK):
            first, spots = places[t]
            for hx in range(2):
                dens = []
                for pos in range(4):
                    own = octs[((first * 2 + hx) * 4 + pos) * 4 + pos].astype(F32)
                    dens.append(own * octs[spots[hx][pos]].astype(F32))
                even0, odd0 = dens[0] + dens[1], dens[0] - dens[1]
                even1, odd1 = dens[2] + dens[3], dens[2] - dens[3]
                folded = (even0 + even1, odd0 + odd1, even0 - even1, odd0 - odd1)
                for cls in range(4):
                    for lh in range(2):
                        grid_work[cls * 2 + lh, pl.ds(hx * half * BLOCK + t, half, stride=BLOCK), :] = (
                            folded[cls][:, lh * 128 : (lh + 1) * 128]
                        )

        def transform(cls, table_ref):
            both = jnp.concatenate([grid_work[cls * 2], grid_work[cls * 2 + 1]], axis=1)
            high, low = halves(both)
            result = jnp.dot(
                jnp.concatenate([high, low, high], axis=1), table_ref[cls], preferred_element_type=F32
            )
            grid_work[cls * 2] = result[:, :128]
            grid_work[cls * 2 + 1] = result[:, 128:]

        for cls in range(4):
            transform(cls, fwd_ref)
        chains = range(8)
        run = [None] * 8
        for x in range(length):
            for ch in chains:
                here = grid_work[ch, x * BLOCK : (x + 1) * BLOCK, :]
                factor = jnp.broadcast_to(fac_ref[ch, x : x + 1, :], (BLOCK, 128))
                run[ch] = (here if x == 0 else here + run[ch]) * factor
                grid_work[ch, x * BLOCK : (x + 1) * BLOCK, :] = run[ch]
        for x in range(length - 2, -1, -1):
            for ch in chains:
                here = grid_work[ch, x * BLOCK : (x + 1) * BLOCK, :]
                factor = jnp.broadcast_to(fac_ref[ch, x : x + 1, :], (BLOCK, 128))
                run[ch] = here + factor * run[ch]
                grid_work[ch, x * BLOCK : (x + 1) * BLOCK, :] = run[ch]
        for cls in range(4):
            transform(cls, bwd_ref)
        for t in range(BLOCK):
            first, spots = places[t]
            for hx in range(2):
                folded = []
                for cls in range(4):
                    folded.append(
                        jnp.concatenate(
                            [
                                grid_work[cls * 2 + lh, pl.ds(hx * half * BLOCK + t, half, stride=BLOCK), :]
                                for lh in range(2)
                            ],
                            axis=1,
                        )
                    )
                sum0, dif0 = folded[0] + folded[1], folded[0] - folded[1]
                sum1, dif1 = folded[2] + folded[3], folded[2] - folded[3]
                potential = (sum0 + sum1, dif0 + dif1, sum0 - sum1, dif0 - dif1)
                for pos in range(4):
                    moved = octs[spots[hx][pos]].astype(F32)
                    totals[first * 8 + hx * 4 + pos] += potential[pos] * moved
        return carry

    lax.fori_loop(0, (live_count + BLOCK - 1) // BLOCK, run_block, 0)

    def send_out(owner, carry):
        top = jnp.abs(totals[owner * 8])
        for k in range(1, 8):
            top = jnp.maximum(top, jnp.abs(totals[owner * 8 + k]))
        top = jnp.maximum(jnp.max(top, axis=0, keepdims=True), 2.0**-110)
        power = jnp.ceil(jnp.log2(top) + 1e-4)
        gain = jnp.exp2(-power) * LEVELS
        for k in range(8):
            level = jnp.round(totals[owner * 8 + k] * gain).astype(jnp.int32).astype(jnp.int16)
            for lh in range(2):
                first = (k * 2 + lh) * half
                out_ref[owner, first : first + half, :] = level[:, lh * 128 : (lh + 1) * 128]
        codes = jnp.concatenate(
            [jnp.broadcast_to(power[:, lh * 128 : (lh + 1) * 128], (8, 128)) for lh in range(2)], axis=0
        )
        out_ref[owner, 16 * half :, :] = codes.astype(jnp.int32).astype(jnp.int16)
        return carry

    lax.fori_loop(0, nodes, send_out, 0)


def final_kernel(wanted_ref, in_ref, table_ref, out_ref, totals, work):
    nodes = in_ref.shape[0]
    orbs = out_ref.shape[0]
    length = work.shape[1] // orbs
    half = length // 2
    area = half * half
    plane = length * length
    totals[...] = jnp.zeros_like(totals)

    def add_one(node, carry):
        target = wanted_ref[node]

        @pl.when(target >= 0)
        def _():
            codes = in_ref[node, 16 * half :, :].astype(jnp.int32).astype(F32)
            for lh in range(2):
                gain = jnp.exp2(codes[lh * 8 : lh * 8 + 1]) * (1.0 / LEVELS)
                for k in range(8):
                    first = (k * 2 + lh) * half
                    level = in_ref[node, first : first + half, :].astype(jnp.int32).astype(F32)
                    hx, pos = k // 4, k % 4
                    totals[pos * 2 + lh, pl.ds(target * length + hx * half, half), :] += level * gain

        return carry

    lax.fori_loop(0, nodes, add_one, 0)
    for py in range(2):
        rows = jnp.concatenate([totals[py * 4 + j] for j in range(4)], axis=1)
        high, low = halves(rows)
        result = jnp.dot(high, table_ref[py], preferred_element_type=F32) + jnp.dot(
            low, table_ref[py], preferred_element_type=F32
        )
        for j in range(4):
            work[py * 4 + j] = result[:, j * 128 : (j + 1) * 128]
    for x in range(length):
        for j in range(plane // 128):
            out_ref[:, x * plane + j * 128 : x * plane + (j + 1) * 128] = work[
                j, pl.ds(x, orbs, stride=length), :
            ]


def on_device(phi, offsets, fetch, task_pairs, task_count):
    nodes = lax.axis_size("orb")
    orbs, volume = phi.shape
    length = cube_root(volume)
    half, plane = length // 2, length * length
    area = half * half
    tables = host_tables(length)
    smem = pl.BlockSpec(memory_space=pltpu.SMEM)
    vmem = pl.BlockSpec(memory_space=pltpu.VMEM)
    params = pltpu.CompilerParams(vmem_limit_bytes=56 << 20)
    packed = pl.pallas_call(
        pack_kernel,
        out_shape=jax.ShapeDtypeStruct((orbs, length, plane), BF16),
        in_specs=[vmem, vmem],
        out_specs=vmem,
        scratch_shapes=[pltpu.VMEM((plane // 128, orbs * length, 128), F32)],
        compiler_params=params,
        name="pack",
    )(phi, tables["pack"])
    asked = lax.all_to_all(fetch.reshape(nodes, 1), "orb", split_axis=0, concat_axis=0, tiled=True)
    wanted = asked[:, 0]
    outgoing = jnp.take(packed, jnp.maximum(wanted, 0), axis=0)
    incoming = lax.all_to_all(outgoing, "orb", split_axis=0, concat_axis=0, tiled=True)
    rows = 16 * half + 16
    partial = pl.pallas_call(
        functools.partial(solve_kernel, orbs),
        out_shape=jax.ShapeDtypeStruct((nodes, rows, 128), jnp.int16),
        in_specs=[smem] * 4 + [vmem] * 5,
        out_specs=vmem,
        scratch_shapes=[
            pltpu.VMEM((nodes * 32 + 1, half, area), BF16),
            pltpu.VMEM((8, length * BLOCK, 128), F32),
            pltpu.VMEM((nodes * 8, half, area), F32),
        ],
        compiler_params=params,
        name="solve",
    )(
        fetch.reshape(-1), offsets.reshape(-1), task_pairs.reshape(-1), task_count, incoming,
        tables["forward"], tables["backward"], tables["factors"], tables["variants"],
    )
    returned = lax.all_to_all(partial, "orb", split_axis=0, concat_axis=0, tiled=True)
    return pl.pallas_call(
        final_kernel,
        out_shape=jax.ShapeDtypeStruct((orbs, volume), F32),
        in_specs=[smem, vmem, vmem],
        out_specs=vmem,
        scratch_shapes=[
            pltpu.VMEM((8, orbs * length, 128), F32),
            pltpu.VMEM((plane // 128, orbs * length, 128), F32),
        ],
        compiler_params=params,
        name="final",
    )(wanted, returned, tables["unpack"])


def solution(mesh):
    in_specs = (
        P(("groups", "orb"), None),
        P("groups", None),
        P(("groups", "orb"), None),
        P(("groups", "orb"), None),
        P(("groups", "orb")),
    )
    out_specs = P(("groups", "orb"), None)
    return jax.shard_map(
        on_device, mesh=mesh, in_specs=in_specs, out_specs=out_specs, check_vma=False
    )
```

```python
import functools

import jax
import jax.numpy as jnp
import ml_dtypes
import numpy as np
from jax import lax
from jax.experimental import pallas as pl
from jax.experimental.pallas import tpu as pltpu
from jax.sharding import PartitionSpec as P

BLOCK = 8
PITCH = 9
LEVELS = 32704.0
BF16 = jnp.bfloat16
F32 = jnp.float32


def cube_root(volume):
    length = 1
    while length * length * length < volume:
        length = length + 1
    return length


def split_bf16(values):
    high = values.astype(ml_dtypes.bfloat16)
    low = (values - high.astype(np.float64)).astype(ml_dtypes.bfloat16)
    return high, low


def host_tables(length):
    half = length // 2
    area = half * half
    count = np.arange(length) + 1.0
    sine = np.sqrt(2.0 / (length + 1)) * np.sin(np.pi * np.outer(count, count) / (length + 1))
    eigen = 2.0 - 2.0 * np.cos(np.pi * count / (length + 1))
    fold = [sine[parity::2, :half].T for parity in (0, 1)]
    forward, backward, factors = [], [], []
    for par_y in (0, 1):
        for par_z in (0, 1):
            table = np.kron(fold[par_y], fold[par_z])
            high, low = split_bf16(table)
            forward.append(np.concatenate([high, high, low], axis=0))
            high, low = split_bf16(table.T)
            backward.append(np.concatenate([high, high, low], axis=0))
            beta = 2.0 + (eigen[par_y::2][:, None] + eigen[par_z::2][None, :]).reshape(area)
            rows = [1.0 / beta]
            for _ in range(half - 1):
                rows.append(1.0 / (beta - rows[-1]))
            rows.append(1.0 / (1.0 - rows[-1] ** 2))
            rows.extend([rows[-1]] * 7)
            rows = np.stack(rows).astype(np.float32)
            factors.append(rows[:, : area // 2])
            factors.append(rows[:, area // 2 :])
    place = np.arange(area)
    low_y, low_z = place // half, place % half
    variants = []
    for rev_y, rev_z in ((0, 1), (1, 0), (1, 1)):
        src_y = half - 1 - low_y if rev_y else low_y
        src_z = half - 1 - low_z if rev_z else low_z
        one_hot = np.zeros((area, area), ml_dtypes.bfloat16)
        one_hot[src_y * half + src_z, place] = 1
        variants.append(one_hot)
    wide = 2 * area
    spot = np.arange(wide)
    pack = np.zeros((wide, wide), ml_dtypes.bfloat16)
    z_half, rest = spot // area, spot % area
    pack[(rest // half) * length + z_half * half + rest % half, spot] = 1
    unpack = []
    for par_y in (0, 1):
        y_nat = half - 1 - rest // half if par_y else rest // half
        z_nat = np.where(z_half == 1, length - 1 - rest % half, rest % half)
        one_hot = np.zeros((wide, wide), ml_dtypes.bfloat16)
        one_hot[spot, y_nat * length + z_nat] = 1
        unpack.append(one_hot)
    return dict(
        forward=np.stack(forward),
        backward=np.stack(backward),
        factors=np.stack(factors),
        variants=np.concatenate(variants, axis=1),
        pack=pack,
        unpack=np.stack(unpack),
    )


def halves(value):
    high = value.astype(BF16)
    low = (value - high.astype(F32)).astype(BF16)
    return high, low


def ask_kernel(fetch_ref, out_ref):
    for node in range(out_ref.shape[0]):
        out_ref[node] = jnp.full(out_ref.shape[1:], fetch_ref[node], jnp.int32)


def pack_kernel(phi_ref, table_ref, out_ref, work):
    orbs = phi_ref.shape[0]
    length = out_ref.shape[1]
    plane = length * length
    wide = plane // 2
    pitch = orbs + 1
    for y_half in range(2):
        rows = jnp.concatenate(
            [phi_ref[:, x * plane + y_half * wide : x * plane + (y_half + 1) * wide] for x in range(length)],
            axis=0,
        )
        moved = jnp.dot(rows, table_ref[...], preferred_element_type=F32)
        for j in range(wide // 128):
            for x in range(length):
                work[y_half * (wide // 128) + j, x * pitch : x * pitch + orbs, :] = moved[
                    x * orbs : (x + 1) * orbs, j * 128 : (j + 1) * 128
                ]
    for orb in range(orbs):
        for j in range(plane // 128):
            piece = work[j, pl.ds(orb, length, stride=pitch), :]
            out_ref[orb, :, j * 128 : (j + 1) * 128] = piece.astype(BF16)


def pick_kernel(asked_ref, packed_ref, out_ref, sems):
    nodes = out_ref.shape[0]
    copies = []
    for node in range(nodes):
        orb = jnp.maximum(asked_ref[node, 0, 0], 0)
        copies.append(pltpu.make_async_copy(packed_ref.at[orb], out_ref.at[node], sems.at[node]))
        copies[-1].start()
    for copy in copies:
        copy.wait()


def solve_kernel(
    orbs, fetch_ref, offsets_ref, pairs_ref, count_ref, in_hbm, var_hbm, fwd_hbm, bwd_hbm, fac_hbm,
    out_hbm, octs, even_work, odd_work, totals, plan, fwd_ref, bwd_ref, fac_ref, var_ref, in_ref,
    out_ref, sems, in_sems, out_sems,
):
    nodes, length = in_ref.shape[0], in_ref.shape[1]
    half = length // 2
    area = half * half
    zero_at = nodes * 32
    group = 8
    sources = ((var_hbm, var_ref), (fwd_hbm, fwd_ref), (bwd_hbm, bwd_ref), (fac_hbm, fac_ref))
    tables = [
        pltpu.make_async_copy(source, target, sems.at[k]) for k, (source, target) in enumerate(sources)
    ]
    def arrival(step):
        spots = pl.ds(step * group, group)
        return pltpu.make_async_copy(in_hbm.at[spots], in_ref.at[spots], in_sems.at[step])

    tables[0].start()
    for step in range(nodes // group):
        arrival(step).start()
    for table in tables[1:]:
        table.start()
    octs[zero_at] = jnp.zeros((half, area), BF16)
    live_count = count_ref[0]
    last_slot = pairs_ref.shape[0] // 2 - 1

    def make_variants(step, carry):
        arrival(step).wait()
        for quad in range(4):
            block = in_ref[pl.ds(step * group, group), :, quad * area : (quad + 1) * area]
            turned = jnp.dot(
                block.reshape(group * length, area), var_ref[...], preferred_element_type=F32
            ).astype(BF16)
            for one in range(group):
                for hx in range(2):
                    base = (((step * group + one) * 2 + hx) * 4 + quad) * 4
                    octs[base] = block[one, hx * half : (hx + 1) * half]
                    first = one * length + hx * half
                    for rev in range(3):
                        octs[base + 1 + rev] = turned[first : first + half, rev * area : (rev + 1) * area]
        return carry

    tables[0].wait()
    lax.fori_loop(0, nodes // group, make_variants, 0)

    def clear(step, carry):
        for k in range(8):
            totals[step * 8 + k] = jnp.zeros((half, area), F32)
        return carry

    lax.fori_loop(0, nodes, clear, 0)
    for ch in range(8):
        even_work[ch] = jnp.zeros(even_work.shape[1:], F32)
        odd_work[ch] = jnp.zeros(odd_work.shape[1:], F32)
    for t in range(BLOCK):
        plan[t * 9] = 0
        for k in range(8):
            plan[t * 9 + 1 + k] = zero_at

    def multiply(work, slot, t):
        at = jnp.minimum(slot, last_slot)
        first, second = pairs_ref[2 * at], pairs_ref[2 * at + 1]
        id_a = first * orbs + jnp.maximum(fetch_ref[first], 0)
        id_b = second * orbs + jnp.maximum(fetch_ref[second], 0)
        shift = [offsets_ref[id_a * 3 + k] - offsets_ref[id_b * 3 + k] for k in range(3)]
        fits = [[(side + shift[k] >= 0) & (side + shift[k] < 2) for side in range(2)] for k in range(3)]
        start = second * 32 + shift[0] * 16 + shift[1] * 8 + shift[2] * 4
        live = slot < live_count
        note = (slot + BLOCK) * 9
        plan[note] = first
        for hx in range(2):
            dens = []
            for pos in range(4):
                py, pz = pos // 2, pos % 2
                inside = live & fits[0][hx] & fits[1][py] & fits[2][pz]
                spot = jnp.where(inside, start + (hx * 16 + py * 8 + pz * 4 + pos), zero_at)
                plan[note + 1 + hx * 4 + pos] = spot
                own = octs[first * 32 + (hx * 16 + pos * 5)].astype(F32)
                dens.append(own * octs[spot].astype(F32))
            even0, odd0 = dens[0] + dens[1], dens[0] - dens[1]
            even1, odd1 = dens[2] + dens[3], dens[2] - dens[3]
            folded = (even0 + even1, odd0 + odd1, even0 - even1, odd0 - odd1)
            for cls in range(4):
                for lh in range(2):
                    work[cls * 2 + lh, pl.ds(hx * half * PITCH + t, half, stride=PITCH), :] = folded[cls][
                        :, lh * 128 : (lh + 1) * 128
                    ]

    def gather(work, slot, t):
        note = (slot + BLOCK) * 9
        first = plan[note] * 8
        for hx in range(2):
            folded = []
            for cls in range(4):
                pieces = [
                    work[cls * 2 + lh, pl.ds(hx * half * PITCH + t, half, stride=PITCH), :] for lh in range(2)
                ]
                folded.append(jnp.concatenate(pieces, axis=1))
            sum0, dif0 = folded[0] + folded[1], folded[0] - folded[1]
            sum1, dif1 = folded[2] + folded[3], folded[2] - folded[3]
            potential = (sum0 + sum1, dif0 + dif1, sum0 - sum1, dif0 - dif1)
            for pos in range(4):
                moved = octs[plan[note + 1 + hx * 4 + pos]].astype(F32)
                totals[first + (hx * 4 + pos)] += potential[pos] * moved

    def begin(work, cls, table_ref):
        both = jnp.concatenate(
            [
                jnp.concatenate(
                    [work[cls * 2 + lh, x * PITCH : x * PITCH + BLOCK, :] for x in range(length)], axis=0
                )
                for lh in range(2)
            ],
            axis=1,
        )
        high, low = halves(both)
        return jnp.dot(
            jnp.concatenate([high, low, high], axis=1), table_ref[cls], preferred_element_type=F32
        )

    def finish(work, cls, result):
        for x in range(length):
            for lh in range(2):
                work[cls * 2 + lh, x * PITCH : x * PITCH + BLOCK, :] = result[
                    x * BLOCK : (x + 1) * BLOCK, lh * 128 : (lh + 1) * 128
                ]

    def sweep(work, chains):
        def rows(x):
            return slice(x * PITCH, x * PITCH + BLOCK)

        def factor(ch, x):
            return jnp.broadcast_to(fac_ref[ch, x : x + 1, :], (BLOCK, 128))

        low, high = {}, {}
        for x in range(half):
            far = length - 1 - x
            for ch in chains:
                scale = factor(ch, x)
                from_low, from_high = work[ch, rows(x), :], work[ch, rows(far), :]
                if x > 0:
                    from_low, from_high = from_low + low[ch], from_high + high[ch]
                low[ch], high[ch] = from_low * scale, from_high * scale
                if x < half - 1:
                    work[ch, rows(x), :] = low[ch]
                    work[ch, rows(far), :] = high[ch]
        for ch in chains:
            scale, meet = factor(ch, half - 1), factor(ch, half)
            low[ch], high[ch] = (low[ch] + scale * high[ch]) * meet, (high[ch] + scale * low[ch]) * meet
            work[ch, rows(half - 1), :] = low[ch]
            work[ch, rows(half), :] = high[ch]
        for x in range(half - 2, -1, -1):
            far = length - 1 - x
            for ch in chains:
                scale = factor(ch, x)
                low[ch] = work[ch, rows(x), :] + scale * low[ch]
                high[ch] = work[ch, rows(far), :] + scale * high[ch]
                work[ch, rows(x), :] = low[ch]
                work[ch, rows(far), :] = high[ch]

    def half_step(work, other, before, after):
        share = BLOCK // 4
        for cls in range(4):
            result = begin(work, cls, fwd_ref)
            for t in range(cls * share, (cls + 1) * share):
                gather(other, before * BLOCK + t, t)
            if cls == 2:
                sweep(work, range(4))
            finish(work, cls, result)
        for cls in range(4):
            result = begin(work, cls, bwd_ref)
            if cls == 0:
                sweep(work, range(4, 8))
            for t in range(cls * share, (cls + 1) * share):
                multiply(other, after * BLOCK + t, t)
            finish(work, cls, result)

    for t in range(BLOCK):
        multiply(even_work, t, t)
    for table in tables[1:]:
        table.wait()

    def run_pair(step, carry):
        half_step(even_work, odd_work, 2 * step - 1, 2 * step + 1)
        half_step(odd_work, even_work, 2 * step, 2 * step + 2)
        return carry

    pairs = (live_count + 2 * BLOCK - 1) // (2 * BLOCK)
    lax.fori_loop(0, pairs, run_pair, 0)
    for t in range(BLOCK):
        gather(odd_work, (2 * pairs - 1) * BLOCK + t, t)

    def send_out(owner, carry):
        top = jnp.abs(totals[owner * 8])
        for k in range(1, 8):
            top = jnp.maximum(top, jnp.abs(totals[owner * 8 + k]))
        top = jnp.maximum(jnp.max(top, axis=0, keepdims=True), 2.0**-110)
        power = jnp.ceil(jnp.log2(top) + 1e-4)
        gain = jnp.exp2(-power) * LEVELS
        for k in range(8):
            level = jnp.round(totals[owner * 8 + k] * gain).astype(jnp.int32).astype(jnp.int16)
            for lh in range(2):
                first = (k * 2 + lh) * half
                out_ref[owner, first : first + half, :] = level[:, lh * 128 : (lh + 1) * 128]
        codes = jnp.concatenate(
            [jnp.broadcast_to(power[:, lh * 128 : (lh + 1) * 128], (8, 128)) for lh in range(2)], axis=0
        )
        out_ref[owner, 16 * half :, :] = codes.astype(jnp.int32).astype(jnp.int16)
        departure(owner).start()
        return carry

    def departure(owner):
        return pltpu.make_async_copy(out_ref.at[owner], out_hbm.at[owner], out_sems.at[owner])

    def leave(owner, carry):
        departure(owner).wait()
        return carry

    lax.fori_loop(0, nodes, send_out, 0)
    lax.fori_loop(0, nodes, leave, 0)


def final_kernel(asked_ref, in_ref, code_ref, table_ref, out_ref, totals, work):
    nodes = in_ref.shape[0]
    orbs, width = out_ref.shape
    half = totals.shape[1] // orbs
    plane = width // half
    pitch = half + 1
    totals[...] = jnp.zeros_like(totals)

    def add_one(node, carry):
        target = asked_ref[node, 0, 0]

        @pl.when(target >= 0)
        def _():
            codes = code_ref[node].astype(jnp.int32).astype(F32)
            start = pl.multiple_of(target * half, half)
            for lh in range(2):
                gain = jnp.exp2(codes[lh * 8 : lh * 8 + 1]) * (1.0 / LEVELS)
                for pos in range(4):
                    first = (pos * 2 + lh) * half
                    level = in_ref[node, first : first + half, :].astype(jnp.int32).astype(F32)
                    totals[pos * 2 + lh, pl.ds(start, half), :] += level * gain

        return carry

    lax.fori_loop(0, nodes, add_one, 0)
    for py in range(2):
        rows = jnp.concatenate([totals[py * 4 + j] for j in range(4)], axis=1)
        high, low = halves(rows)
        result = jnp.dot(high, table_ref[py], preferred_element_type=F32) + jnp.dot(
            low, table_ref[py], preferred_element_type=F32
        )
        for j in range(4):
            for orb in range(orbs):
                work[py * 4 + j, orb * pitch : orb * pitch + half, :] = result[
                    orb * half : (orb + 1) * half, j * 128 : (j + 1) * 128
                ]
    for x in range(half):
        for j in range(plane // 128):
            out_ref[:, x * plane + j * 128 : x * plane + (j + 1) * 128] = work[
                j, pl.ds(x, orbs, stride=pitch), :
            ]


def call_solve(orbs, fetch, offsets, pairs, count, incoming):
    nodes, length, plane = incoming.shape
    half = length // 2
    area = half * half
    tables = host_tables(length)
    smem = pl.BlockSpec(memory_space=pltpu.SMEM)
    hbm = pl.BlockSpec(memory_space=pl.ANY)
    work = pltpu.VMEM((8, length * PITCH, 128), F32)
    steps = (pairs.shape[0] // 2 + 2 * BLOCK - 1) // (2 * BLOCK)
    return pl.pallas_call(
        functools.partial(solve_kernel, orbs),
        out_shape=jax.ShapeDtypeStruct((nodes, 16 * half + 16, 128), jnp.int16),
        in_specs=[smem] * 4 + [hbm] * 5,
        out_specs=hbm,
        scratch_shapes=[
            pltpu.VMEM((nodes * 32 + 1, half, area), BF16),
            work,
            work,
            pltpu.VMEM((nodes * 8, half, area), F32),
            pltpu.SMEM(((2 * steps + 2) * BLOCK * 9,), jnp.int32),
            pltpu.VMEM((4, 3 * area, area), BF16),
            pltpu.VMEM((4, 3 * area, area), BF16),
            pltpu.VMEM((8, half + 8, 128), F32),
            pltpu.VMEM((area, 3 * area), BF16),
            pltpu.VMEM((nodes, length, plane), BF16),
            pltpu.VMEM((nodes, 16 * half + 16, 128), jnp.int16),
            pltpu.SemaphoreType.DMA((4,)),
            pltpu.SemaphoreType.DMA((nodes // 8,)),
            pltpu.SemaphoreType.DMA((nodes,)),
        ],
        compiler_params=pltpu.CompilerParams(vmem_limit_bytes=56 << 20),
        name="solve",
    )(
        fetch, offsets, pairs, count, incoming,
        tables["variants"], tables["forward"], tables["backward"], tables["factors"],
    )


def on_device(phi, offsets, fetch, task_pairs, task_count):
    nodes = lax.axis_size("orb")
    orbs, volume = phi.shape
    length = cube_root(volume)
    half, plane = length // 2, length * length
    tables = host_tables(length)
    smem = pl.BlockSpec(memory_space=pltpu.SMEM)
    vmem = pl.BlockSpec(memory_space=pltpu.VMEM)
    hbm = pl.BlockSpec(memory_space=pl.ANY)
    params = pltpu.CompilerParams(vmem_limit_bytes=56 << 20)
    fetch = fetch.reshape(-1)
    asking = pl.pallas_call(
        ask_kernel,
        out_shape=jax.ShapeDtypeStruct((nodes, 1, 128), jnp.int32),
        in_specs=[smem],
        out_specs=vmem,
        name="ask",
    )(fetch)
    packed = pl.pallas_call(
        pack_kernel,
        out_shape=jax.ShapeDtypeStruct((orbs, length, plane), BF16),
        in_specs=[vmem, vmem],
        out_specs=vmem,
        scratch_shapes=[pltpu.VMEM((plane // 128, (orbs + 1) * length, 128), F32)],
        compiler_params=params,
        name="pack",
    )(phi, tables["pack"])
    asked = lax.all_to_all(asking, "orb", split_axis=0, concat_axis=0, tiled=True)
    outgoing = pl.pallas_call(
        pick_kernel,
        out_shape=jax.ShapeDtypeStruct((nodes, length, plane), BF16),
        in_specs=[smem, hbm],
        out_specs=hbm,
        scratch_shapes=[pltpu.SemaphoreType.DMA((nodes,))],
        name="pick",
    )(asked, packed)
    incoming = lax.all_to_all(outgoing, "orb", split_axis=0, concat_axis=0, tiled=True)
    partial = call_solve(
        orbs, fetch, offsets.reshape(-1), task_pairs.reshape(-1), task_count, incoming
    )
    returned = lax.all_to_all(partial, "orb", split_axis=0, concat_axis=0, tiled=True)
    return pl.pallas_call(
        final_kernel,
        grid=(2,),
        out_shape=jax.ShapeDtypeStruct((orbs, volume), F32),
        in_specs=[
            smem,
            pl.BlockSpec((nodes, 8 * half, 128), lambda hx: (0, hx, 0)),
            pl.BlockSpec((nodes, 16, 128), lambda hx: (0, half, 0)),
            pl.BlockSpec((2, plane // 2, plane // 2), lambda hx: (0, 0, 0)),
        ],
        out_specs=pl.BlockSpec((orbs, volume // 2), lambda hx: (0, hx)),
        scratch_shapes=[
            pltpu.VMEM((8, orbs * half, 128), F32),
            pltpu.VMEM((plane // 128, orbs * (half + 1), 128), F32),
        ],
        compiler_params=params,
        name="final",
    )(asked, returned, returned, tables["unpack"])


def solution(mesh):
    in_specs = (
        P(("groups", "orb"), None),
        P("groups", None),
        P(("groups", "orb"), None),
        P(("groups", "orb"), None),
        P(("groups", "orb")),
    )
    out_specs = P(("groups", "orb"), None)
    return jax.shard_map(
        on_device, mesh=mesh, in_specs=in_specs, out_specs=out_specs, check_vma=False
    )
```

```python
import functools

import jax
import jax.numpy as jnp
import ml_dtypes
import numpy as np
from jax import lax
from jax.experimental import pallas as pl
from jax.experimental.pallas import tpu as pltpu
from jax.sharding import PartitionSpec as P

BLOCK = 8
PITCH = 9
LEVELS = 32704.0
BF16 = jnp.bfloat16
F32 = jnp.float32


def cube_root(volume):
    length = 1
    while length * length * length < volume:
        length = length + 1
    return length


def split_bf16(values):
    high = values.astype(ml_dtypes.bfloat16)
    low = (values - high.astype(np.float64)).astype(ml_dtypes.bfloat16)
    return high, low


def host_tables(length):
    half = length // 2
    area = half * half
    count = np.arange(length) + 1.0
    sine = np.sqrt(2.0 / (length + 1)) * np.sin(np.pi * np.outer(count, count) / (length + 1))
    eigen = 2.0 - 2.0 * np.cos(np.pi * count / (length + 1))
    fold = [sine[parity::2, :half].T for parity in (0, 1)]
    forward, backward, factors = [], [], []
    for par_y in (0, 1):
        for par_z in (0, 1):
            table = np.kron(fold[par_y], fold[par_z])
            high, low = split_bf16(table)
            forward.append(np.concatenate([high, high, low], axis=0))
            high, low = split_bf16(table.T)
            backward.append(np.concatenate([high, high, low], axis=0))
            beta = 2.0 + (eigen[par_y::2][:, None] + eigen[par_z::2][None, :]).reshape(area)
            rows = [1.0 / beta]
            for _ in range(half - 1):
                rows.append(1.0 / (beta - rows[-1]))
            rows.append(1.0 / (1.0 - rows[-1] ** 2))
            rows.extend([rows[-1]] * 7)
            rows = np.stack(rows).astype(np.float32)
            factors.append(rows[:, : area // 2])
            factors.append(rows[:, area // 2 :])
    place = np.arange(area)
    low_y, low_z = place // half, place % half
    variants = []
    for rev_y, rev_z in ((0, 1), (1, 0), (1, 1)):
        src_y = half - 1 - low_y if rev_y else low_y
        src_z = half - 1 - low_z if rev_z else low_z
        one_hot = np.zeros((area, area), ml_dtypes.bfloat16)
        one_hot[src_y * half + src_z, place] = 1
        variants.append(one_hot)
    wide = 2 * area
    spot = np.arange(wide)
    pack = np.zeros((wide, wide), ml_dtypes.bfloat16)
    z_half, rest = spot // area, spot % area
    pack[(rest // half) * length + z_half * half + rest % half, spot] = 1
    unpack = []
    for par_y in (0, 1):
        y_nat = half - 1 - rest // half if par_y else rest // half
        z_nat = np.where(z_half == 1, length - 1 - rest % half, rest % half)
        one_hot = np.zeros((wide, wide), ml_dtypes.bfloat16)
        one_hot[spot, y_nat * length + z_nat] = 1
        unpack.append(one_hot)
    return dict(
        forward=np.stack(forward),
        backward=np.stack(backward),
        factors=np.stack(factors),
        variants=np.concatenate(variants, axis=1),
        pack=pack,
        unpack=np.stack(unpack),
    )


def halves(value):
    high = value.astype(BF16)
    low = (value - high.astype(F32)).astype(BF16)
    return high, low


def ask_kernel(fetch_ref, out_ref):
    for node in range(out_ref.shape[0]):
        out_ref[node] = jnp.full(out_ref.shape[1:], fetch_ref[node], jnp.int32)


def pack_kernel(phi_ref, table_ref, out_ref, work):
    orbs = phi_ref.shape[0]
    length = out_ref.shape[1]
    plane = length * length
    wide = plane // 2
    pitch = orbs + 1
    for y_half in range(2):
        rows = jnp.concatenate(
            [phi_ref[:, x * plane + y_half * wide : x * plane + (y_half + 1) * wide] for x in range(length)],
            axis=0,
        )
        moved = jnp.dot(rows, table_ref[...], preferred_element_type=F32)
        for j in range(wide // 128):
            for x in range(length):
                work[y_half * (wide // 128) + j, x * pitch : x * pitch + orbs, :] = moved[
                    x * orbs : (x + 1) * orbs, j * 128 : (j + 1) * 128
                ]
    for orb in range(orbs):
        for j in range(plane // 128):
            piece = work[j, pl.ds(orb, length, stride=pitch), :]
            out_ref[orb, :, j * 128 : (j + 1) * 128] = piece.astype(BF16)


def pick_kernel(asked_ref, packed_ref, out_ref):
    for node in range(out_ref.shape[0]):
        out_ref[node] = packed_ref[jnp.maximum(asked_ref[node, 0, 0], 0)]


def solve_kernel(
    orbs, fetch_ref, offsets_ref, pairs_ref, count_ref, in_ref, var_ref, fwd_hbm, bwd_hbm, fac_hbm,
    out_ref, octs, even_work, odd_work, totals, plan, fwd_ref, bwd_ref, fac_ref, sems,
):
    nodes, length = in_ref.shape[0], in_ref.shape[1]
    half = length // 2
    area = half * half
    zero_at = nodes * 32
    group = 8
    sources = ((fwd_hbm, fwd_ref), (bwd_hbm, bwd_ref), (fac_hbm, fac_ref))
    tables = [
        pltpu.make_async_copy(source, target, sems.at[k]) for k, (source, target) in enumerate(sources)
    ]
    for table in tables:
        table.start()
    octs[zero_at] = jnp.zeros((half, area), BF16)
    live_count = count_ref[0]
    last_slot = pairs_ref.shape[0] // 2 - 1

    def make_variants(step, carry):
        for quad in range(4):
            block = in_ref[pl.ds(step * group, group), :, quad * area : (quad + 1) * area]
            turned = jnp.dot(
                block.reshape(group * length, area), var_ref[...], preferred_element_type=F32
            ).astype(BF16)
            for one in range(group):
                for hx in range(2):
                    base = (((step * group + one) * 2 + hx) * 4 + quad) * 4
                    octs[base] = block[one, hx * half : (hx + 1) * half]
                    first = one * length + hx * half
                    for rev in range(3):
                        octs[base + 1 + rev] = turned[first : first + half, rev * area : (rev + 1) * area]
        return carry

    lax.fori_loop(0, nodes // group, make_variants, 0)

    def clear(step, carry):
        for k in range(8):
            totals[step * 8 + k] = jnp.zeros((half, area), F32)
        return carry

    lax.fori_loop(0, nodes, clear, 0)
    for ch in range(8):
        even_work[ch] = jnp.zeros(even_work.shape[1:], F32)
        odd_work[ch] = jnp.zeros(odd_work.shape[1:], F32)
    for t in range(BLOCK):
        plan[t * 9] = 0
        for k in range(8):
            plan[t * 9 + 1 + k] = zero_at

    def multiply(work, slot, t):
        at = jnp.minimum(slot, last_slot)
        first, second = pairs_ref[2 * at], pairs_ref[2 * at + 1]
        id_a = first * orbs + jnp.maximum(fetch_ref[first], 0)
        id_b = second * orbs + jnp.maximum(fetch_ref[second], 0)
        shift = [offsets_ref[id_a * 3 + k] - offsets_ref[id_b * 3 + k] for k in range(3)]
        fits = [[(side + shift[k] >= 0) & (side + shift[k] < 2) for side in range(2)] for k in range(3)]
        start = second * 32 + shift[0] * 16 + shift[1] * 8 + shift[2] * 4
        live = slot < live_count
        note = (slot + BLOCK) * 9
        plan[note] = first
        for hx in range(2):
            dens = []
            for pos in range(4):
                py, pz = pos // 2, pos % 2
                inside = live & fits[0][hx] & fits[1][py] & fits[2][pz]
                spot = jnp.where(inside, start + (hx * 16 + py * 8 + pz * 4 + pos), zero_at)
                plan[note + 1 + hx * 4 + pos] = spot
                own = octs[first * 32 + (hx * 16 + pos * 5)].astype(F32)
                dens.append(own * octs[spot].astype(F32))
            even0, odd0 = dens[0] + dens[1], dens[0] - dens[1]
            even1, odd1 = dens[2] + dens[3], dens[2] - dens[3]
            folded = (even0 + even1, odd0 + odd1, even0 - even1, odd0 - odd1)
            for cls in range(4):
                for lh in range(2):
                    work[cls * 2 + lh, pl.ds(hx * half * PITCH + t, half, stride=PITCH), :] = folded[cls][
                        :, lh * 128 : (lh + 1) * 128
                    ]

    def gather(work, slot, t):
        note = (slot + BLOCK) * 9
        first = plan[note] * 8
        for hx in range(2):
            folded = []
            for cls in range(4):
                pieces = [
                    work[cls * 2 + lh, pl.ds(hx * half * PITCH + t, half, stride=PITCH), :] for lh in range(2)
                ]
                folded.append(jnp.concatenate(pieces, axis=1))
            sum0, dif0 = folded[0] + folded[1], folded[0] - folded[1]
            sum1, dif1 = folded[2] + folded[3], folded[2] - folded[3]
            potential = (sum0 + sum1, dif0 + dif1, sum0 - sum1, dif0 - dif1)
            for pos in range(4):
                moved = octs[plan[note + 1 + hx * 4 + pos]].astype(F32)
                totals[first + (hx * 4 + pos)] += potential[pos] * moved

    def begin(work, cls, table_ref):
        both = jnp.concatenate(
            [
                jnp.concatenate(
                    [work[cls * 2 + lh, x * PITCH : x * PITCH + BLOCK, :] for x in range(length)], axis=0
                )
                for lh in range(2)
            ],
            axis=1,
        )
        high, low = halves(both)
        return jnp.dot(
            jnp.concatenate([high, low, high], axis=1), table_ref[cls], preferred_element_type=F32
        )

    def finish(work, cls, result):
        for x in range(length):
            for lh in range(2):
                work[cls * 2 + lh, x * PITCH : x * PITCH + BLOCK, :] = result[
                    x * BLOCK : (x + 1) * BLOCK, lh * 128 : (lh + 1) * 128
                ]

    def sweep(work, chains):
        def rows(x):
            return slice(x * PITCH, x * PITCH + BLOCK)

        def factor(ch, x):
            return jnp.broadcast_to(fac_ref[ch, x : x + 1, :], (BLOCK, 128))

        low, high = {}, {}
        for x in range(half):
            far = length - 1 - x
            for ch in chains:
                scale = factor(ch, x)
                from_low, from_high = work[ch, rows(x), :], work[ch, rows(far), :]
                if x > 0:
                    from_low, from_high = from_low + low[ch], from_high + high[ch]
                low[ch], high[ch] = from_low * scale, from_high * scale
                if x < half - 1:
                    work[ch, rows(x), :] = low[ch]
                    work[ch, rows(far), :] = high[ch]
        for ch in chains:
            scale, meet = factor(ch, half - 1), factor(ch, half)
            low[ch], high[ch] = (low[ch] + scale * high[ch]) * meet, (high[ch] + scale * low[ch]) * meet
            work[ch, rows(half - 1), :] = low[ch]
            work[ch, rows(half), :] = high[ch]
        for x in range(half - 2, -1, -1):
            far = length - 1 - x
            for ch in chains:
                scale = factor(ch, x)
                low[ch] = work[ch, rows(x), :] + scale * low[ch]
                high[ch] = work[ch, rows(far), :] + scale * high[ch]
                work[ch, rows(x), :] = low[ch]
                work[ch, rows(far), :] = high[ch]

    def half_step(work, other, before, after):
        share = BLOCK // 4
        for cls in range(4):
            result = begin(work, cls, fwd_ref)
            for t in range(cls * share, (cls + 1) * share):
                gather(other, before * BLOCK + t, t)
            if cls == 2:
                sweep(work, range(4))
            finish(work, cls, result)
        for cls in range(4):
            result = begin(work, cls, bwd_ref)
            if cls == 0:
                sweep(work, range(4, 8))
            for t in range(cls * share, (cls + 1) * share):
                multiply(other, after * BLOCK + t, t)
            finish(work, cls, result)

    for t in range(BLOCK):
        multiply(even_work, t, t)
    for table in tables:
        table.wait()

    def run_pair(step, carry):
        half_step(even_work, odd_work, 2 * step - 1, 2 * step + 1)
        half_step(odd_work, even_work, 2 * step, 2 * step + 2)
        return carry

    pairs = (live_count + 2 * BLOCK - 1) // (2 * BLOCK)
    lax.fori_loop(0, pairs, run_pair, 0)
    for t in range(BLOCK):
        gather(odd_work, (2 * pairs - 1) * BLOCK + t, t)

    def send_out(owner, carry):
        top = jnp.abs(totals[owner * 8])
        for k in range(1, 8):
            top = jnp.maximum(top, jnp.abs(totals[owner * 8 + k]))
        top = jnp.maximum(jnp.max(top, axis=0, keepdims=True), 2.0**-110)
        power = jnp.ceil(jnp.log2(top) + 1e-4)
        gain = jnp.exp2(-power) * LEVELS
        for k in range(8):
            level = jnp.round(totals[owner * 8 + k] * gain).astype(jnp.int32).astype(jnp.int16)
            for lh in range(2):
                first = (k * 2 + lh) * half
                out_ref[owner, first : first + half, :] = level[:, lh * 128 : (lh + 1) * 128]
        codes = jnp.concatenate(
            [jnp.broadcast_to(power[:, lh * 128 : (lh + 1) * 128], (8, 128)) for lh in range(2)], axis=0
        )
        out_ref[owner, 16 * half :, :] = codes.astype(jnp.int32).astype(jnp.int16)
        return carry

    lax.fori_loop(0, nodes, send_out, 0)


def final_kernel(asked_ref, in_ref, code_ref, table_ref, out_ref, totals, work):
    nodes = in_ref.shape[0]
    orbs, width = out_ref.shape
    half = totals.shape[1] // orbs
    plane = width // half
    pitch = half + 1
    totals[...] = jnp.zeros_like(totals)

    def add_one(node, carry):
        target = asked_ref[node, 0, 0]

        @pl.when(target >= 0)
        def _():
            codes = code_ref[node].astype(jnp.int32).astype(F32)
            start = pl.multiple_of(target * half, half)
            for lh in range(2):
                gain = jnp.exp2(codes[lh * 8 : lh * 8 + 1]) * (1.0 / LEVELS)
                for pos in range(4):
                    first = (pos * 2 + lh) * half
                    level = in_ref[node, first : first + half, :].astype(jnp.int32).astype(F32)
                    totals[pos * 2 + lh, pl.ds(start, half), :] += level * gain

        return carry

    lax.fori_loop(0, nodes, add_one, 0)
    for py in range(2):
        rows = jnp.concatenate([totals[py * 4 + j] for j in range(4)], axis=1)
        high, low = halves(rows)
        result = jnp.dot(high, table_ref[py], preferred_element_type=F32) + jnp.dot(
            low, table_ref[py], preferred_element_type=F32
        )
        for j in range(4):
            for orb in range(orbs):
                work[py * 4 + j, orb * pitch : orb * pitch + half, :] = result[
                    orb * half : (orb + 1) * half, j * 128 : (j + 1) * 128
                ]
    for x in range(half):
        for j in range(plane // 128):
            out_ref[:, x * plane + j * 128 : x * plane + (j + 1) * 128] = work[
                j, pl.ds(x, orbs, stride=pitch), :
            ]


def call_solve(orbs, fetch, offsets, pairs, count, incoming):
    nodes, length, plane = incoming.shape
    half = length // 2
    area = half * half
    tables = host_tables(length)
    smem = pl.BlockSpec(memory_space=pltpu.SMEM)
    hbm = pl.BlockSpec(memory_space=pl.ANY)
    work = pltpu.VMEM((8, length * PITCH, 128), F32)
    steps = (pairs.shape[0] // 2 + 2 * BLOCK - 1) // (2 * BLOCK)
    return pl.pallas_call(
        functools.partial(solve_kernel, orbs),
        out_shape=jax.ShapeDtypeStruct((nodes, 16 * half + 16, 128), jnp.int16),
        in_specs=[smem] * 4 + [pl.BlockSpec(memory_space=pltpu.VMEM)] * 2 + [hbm] * 3,
        out_specs=pl.BlockSpec(memory_space=pltpu.VMEM),
        scratch_shapes=[
            pltpu.VMEM((nodes * 32 + 1, half, area), BF16),
            work,
            work,
            pltpu.VMEM((nodes * 8, half, area), F32),
            pltpu.SMEM(((2 * steps + 2) * BLOCK * 9,), jnp.int32),
            pltpu.VMEM((4, 3 * area, area), BF16),
            pltpu.VMEM((4, 3 * area, area), BF16),
            pltpu.VMEM((8, half + 8, 128), F32),
            pltpu.SemaphoreType.DMA((3,)),
        ],
        compiler_params=pltpu.CompilerParams(vmem_limit_bytes=(10 << 20) + nodes * (704 << 10)),
        name="solve",
    )(
        fetch, offsets, pairs, count, incoming,
        tables["variants"], tables["forward"], tables["backward"], tables["factors"],
    )


def on_device(phi, offsets, fetch, task_pairs, task_count):
    nodes = lax.axis_size("orb")
    orbs, volume = phi.shape
    length = cube_root(volume)
    half, plane = length // 2, length * length
    tables = host_tables(length)
    smem = pl.BlockSpec(memory_space=pltpu.SMEM)
    vmem = pl.BlockSpec(memory_space=pltpu.VMEM)
    params = pltpu.CompilerParams(vmem_limit_bytes=(12 << 20) + nodes * (384 << 10))
    fetch = fetch.reshape(-1)
    asking = pl.pallas_call(
        ask_kernel,
        out_shape=jax.ShapeDtypeStruct((nodes, 1, 128), jnp.int32),
        in_specs=[smem],
        out_specs=vmem,
        name="ask",
    )(fetch)
    packed = pl.pallas_call(
        pack_kernel,
        out_shape=jax.ShapeDtypeStruct((orbs, length, plane), BF16),
        in_specs=[vmem, vmem],
        out_specs=vmem,
        scratch_shapes=[pltpu.VMEM((plane // 128, (orbs + 1) * length, 128), F32)],
        compiler_params=params,
        name="pack",
    )(phi, tables["pack"])
    asked = lax.all_to_all(asking, "orb", split_axis=0, concat_axis=0, tiled=True)
    outgoing = pl.pallas_call(
        pick_kernel,
        out_shape=jax.ShapeDtypeStruct((nodes, length, plane), BF16),
        in_specs=[smem, vmem],
        out_specs=vmem,
        compiler_params=params,
        name="pick",
    )(asked, packed)
    incoming = lax.all_to_all(outgoing, "orb", split_axis=0, concat_axis=0, tiled=True)
    partial = call_solve(
        orbs, fetch, offsets.reshape(-1), task_pairs.reshape(-1), task_count, incoming
    )
    returned = lax.all_to_all(partial, "orb", split_axis=0, concat_axis=0, tiled=True)
    return pl.pallas_call(
        final_kernel,
        grid=(2,),
        out_shape=jax.ShapeDtypeStruct((orbs, volume), F32),
        in_specs=[
            smem,
            pl.BlockSpec((nodes, 8 * half, 128), lambda hx: (0, hx, 0)),
            pl.BlockSpec((nodes, 16, 128), lambda hx: (0, half, 0)),
            pl.BlockSpec((2, plane // 2, plane // 2), lambda hx: (0, 0, 0)),
        ],
        out_specs=pl.BlockSpec((orbs, volume // 2), lambda hx: (0, hx)),
        scratch_shapes=[
            pltpu.VMEM((8, orbs * half, 128), F32),
            pltpu.VMEM((plane // 128, orbs * (half + 1), 128), F32),
        ],
        compiler_params=params,
        name="final",
    )(asked, returned, returned, tables["unpack"])


def solution(mesh):
    in_specs = (
        P(("groups", "orb"), None),
        P("groups", None),
        P(("groups", "orb"), None),
        P(("groups", "orb"), None),
        P(("groups", "orb")),
    )
    out_specs = P(("groups", "orb"), None)
    return jax.shard_map(
        on_device, mesh=mesh, in_specs=in_specs, out_specs=out_specs, check_vma=False
    )
```

```python
import functools

import jax
import jax.numpy as jnp
import ml_dtypes
import numpy as np
from jax import lax
from jax.experimental import pallas as pl
from jax.experimental.pallas import tpu as pltpu
from jax.sharding import PartitionSpec as P

BLOCK = 8
PITCH = 9
LEVELS = 32704.0
BF16 = jnp.bfloat16
F32 = jnp.float32


def cube_root(volume):
    length = 1
    while length * length * length < volume:
        length = length + 1
    return length


def split_bf16(values):
    high = values.astype(ml_dtypes.bfloat16)
    low = (values - high.astype(np.float64)).astype(ml_dtypes.bfloat16)
    return high, low


def host_tables(length):
    half = length // 2
    area = half * half
    count = np.arange(length) + 1.0
    sine = np.sqrt(2.0 / (length + 1)) * np.sin(np.pi * np.outer(count, count) / (length + 1))
    eigen = 2.0 - 2.0 * np.cos(np.pi * count / (length + 1))
    fold = [sine[parity::2, :half].T for parity in (0, 1)]
    forward, backward, factors = [], [], []
    for par_y in (0, 1):
        for par_z in (0, 1):
            table = np.kron(fold[par_y], fold[par_z])
            high, low = split_bf16(table)
            forward.append(np.concatenate([high, low], axis=0))
            high, low = split_bf16(table.T)
            backward.append(np.concatenate([high, low], axis=0))
            beta = 2.0 + (eigen[par_y::2][:, None] + eigen[par_z::2][None, :]).reshape(area)
            rows = [1.0 / beta]
            for _ in range(half - 1):
                rows.append(1.0 / (beta - rows[-1]))
            rows.append(1.0 / (1.0 - rows[-1] ** 2))
            rows.extend([rows[-1]] * 7)
            rows = np.stack(rows).astype(np.float32)
            factors.append(rows[:, : area // 2])
            factors.append(rows[:, area // 2 :])
    place = np.arange(area)
    low_y, low_z = place // half, place % half
    variants = []
    for rev_y, rev_z in ((0, 1), (1, 0), (1, 1)):
        src_y = half - 1 - low_y if rev_y else low_y
        src_z = half - 1 - low_z if rev_z else low_z
        one_hot = np.zeros((area, area), ml_dtypes.bfloat16)
        one_hot[src_y * half + src_z, place] = 1
        variants.append(one_hot)
    wide = 2 * area
    spot = np.arange(wide)
    pack = np.zeros((wide, wide), ml_dtypes.bfloat16)
    z_half, rest = spot // area, spot % area
    pack[(rest // half) * length + z_half * half + rest % half, spot] = 1
    unpack = []
    for par_y in (0, 1):
        y_nat = half - 1 - rest // half if par_y else rest // half
        z_nat = np.where(z_half == 1, length - 1 - rest % half, rest % half)
        one_hot = np.zeros((wide, wide), ml_dtypes.bfloat16)
        one_hot[spot, y_nat * length + z_nat] = 1
        unpack.append(one_hot)
    return dict(
        sines=np.stack([np.stack(forward), np.stack(backward)]),
        factors=np.stack(factors),
        variants=np.concatenate(variants, axis=1),
        pack=pack,
        unpack=np.stack(unpack),
    )


def halves(value):
    high = value.astype(BF16)
    low = (value - high.astype(F32)).astype(BF16)
    return high, low


def ask_kernel(fetch_ref, out_ref):
    for node in range(out_ref.shape[0]):
        out_ref[node] = jnp.full(out_ref.shape[1:], fetch_ref[node], jnp.int32)


def pack_kernel(phi_ref, table_ref, out_ref, work):
    orbs = phi_ref.shape[0]
    length = out_ref.shape[1]
    plane = length * length
    wide = plane // 2
    pitch = orbs + 1
    for y_half in range(2):
        rows = jnp.concatenate(
            [phi_ref[:, x * plane + y_half * wide : x * plane + (y_half + 1) * wide] for x in range(length)],
            axis=0,
        )
        moved = jnp.dot(rows, table_ref[...], preferred_element_type=F32)
        for j in range(wide // 128):
            for x in range(length):
                work[y_half * (wide // 128) + j, x * pitch : x * pitch + orbs, :] = moved[
                    x * orbs : (x + 1) * orbs, j * 128 : (j + 1) * 128
                ]
    for orb in range(orbs):
        for j in range(plane // 128):
            piece = work[j, pl.ds(orb, length, stride=pitch), :]
            out_ref[orb, :, j * 128 : (j + 1) * 128] = piece.astype(BF16)


def pick_kernel(asked_ref, packed_ref, out_ref, sems):
    copies = []
    for node in range(out_ref.shape[0]):
        orb = jnp.maximum(asked_ref[node, 0, 0], 0)
        copies.append(pltpu.make_async_copy(packed_ref.at[orb], out_ref.at[node], sems.at[node]))
        copies[-1].start()
    for copy in copies:
        copy.wait()


def solve_kernel(
    orbs, fetch_ref, offsets_ref, pairs_ref, count_ref, in_ref, var_ref, sine_hbm, fac_hbm,
    out_ref, octs, even_work, odd_work, totals, plan, used, fwd_ref, bwd_ref, fac_ref, sems,
):
    nodes, length = in_ref.shape[0], in_ref.shape[1]
    half = length // 2
    area = half * half
    zero_at = nodes * 32
    group = 8
    area_rows = [pl.ds(0, area), pl.ds(area, area), pl.ds(2 * area, area)]
    moves = [(fac_hbm, fac_ref)]
    for way, target in enumerate((fwd_ref, bwd_ref)):
        for part in range(3):
            source = sine_hbm.at[way, :, area_rows[part // 2], :]
            moves.append((source, target.at[:, area_rows[part], :]))
    tables = [pltpu.make_async_copy(*move, sems.at[k]) for k, move in enumerate(moves)]
    for table in tables:
        table.start()
    octs[zero_at] = jnp.zeros((half, area), BF16)
    live_count = count_ref[0]
    last_slot = pairs_ref.shape[0] // 2 - 1

    def make_variants(step, carry):
        for quad in range(4):
            block = in_ref[pl.ds(step * group, group), :, quad * area : (quad + 1) * area]
            turned = jnp.dot(
                block.reshape(group * length, area), var_ref[...], preferred_element_type=F32
            ).astype(BF16)
            for one in range(group):
                for hx in range(2):
                    base = (((step * group + one) * 2 + hx) * 4 + quad) * 4
                    octs[base] = block[one, hx * half : (hx + 1) * half]
                    first = one * length + hx * half
                    for rev in range(3):
                        octs[base + 1 + rev] = turned[first : first + half, rev * area : (rev + 1) * area]
        return carry

    lax.fori_loop(0, nodes // group, make_variants, 0)

    def clear(step, carry):
        for k in range(8):
            totals[step * 8 + k] = jnp.zeros((half, area), F32)
        used[step] = 0
        return carry

    lax.fori_loop(0, nodes, clear, 0)
    for ch in range(8):
        even_work[ch] = jnp.zeros(even_work.shape[1:], F32)
        odd_work[ch] = jnp.zeros(odd_work.shape[1:], F32)
    for t in range(BLOCK):
        plan[t * 9] = 0
        for k in range(8):
            plan[t * 9 + 1 + k] = zero_at

    def multiply(work, slot, t):
        at = jnp.minimum(slot, last_slot)
        first, second = pairs_ref[2 * at], pairs_ref[2 * at + 1]
        id_a = first * orbs + jnp.maximum(fetch_ref[first], 0)
        id_b = second * orbs + jnp.maximum(fetch_ref[second], 0)
        shift = [offsets_ref[id_a * 3 + k] - offsets_ref[id_b * 3 + k] for k in range(3)]
        fits = [[(side + shift[k] >= 0) & (side + shift[k] < 2) for side in range(2)] for k in range(3)]
        start = second * 32 + shift[0] * 16 + shift[1] * 8 + shift[2] * 4
        live = slot < live_count
        note = (slot + BLOCK) * 9
        plan[note] = first
        used[first] = jnp.where(live, 1, used[first])
        for hx in range(2):
            dens = []
            for pos in range(4):
                py, pz = pos // 2, pos % 2
                inside = live & fits[0][hx] & fits[1][py] & fits[2][pz]
                spot = jnp.where(inside, start + (hx * 16 + py * 8 + pz * 4 + pos), zero_at)
                plan[note + 1 + hx * 4 + pos] = spot
                own = octs[first * 32 + (hx * 16 + pos * 5)].astype(F32)
                dens.append(own * octs[spot].astype(F32))
            even0, odd0 = dens[0] + dens[1], dens[0] - dens[1]
            even1, odd1 = dens[2] + dens[3], dens[2] - dens[3]
            folded = (even0 + even1, odd0 + odd1, even0 - even1, odd0 - odd1)
            for cls in range(4):
                for lh in range(2):
                    work[cls * 2 + lh, pl.ds(hx * half * PITCH + t, half, stride=PITCH), :] = folded[cls][
                        :, lh * 128 : (lh + 1) * 128
                    ]

    def gather(work, slot, t):
        note = (slot + BLOCK) * 9
        first = plan[note] * 8
        for hx in range(2):
            folded = []
            for cls in range(4):
                pieces = [
                    work[cls * 2 + lh, pl.ds(hx * half * PITCH + t, half, stride=PITCH), :] for lh in range(2)
                ]
                folded.append(jnp.concatenate(pieces, axis=1))
            sum0, dif0 = folded[0] + folded[1], folded[0] - folded[1]
            sum1, dif1 = folded[2] + folded[3], folded[2] - folded[3]
            potential = (sum0 + sum1, dif0 + dif1, sum0 - sum1, dif0 - dif1)
            for pos in range(4):
                moved = octs[plan[note + 1 + hx * 4 + pos]].astype(F32)
                totals[first + (hx * 4 + pos)] += potential[pos] * moved

    def begin(work, cls, table_ref):
        both = jnp.concatenate(
            [
                jnp.concatenate(
                    [work[cls * 2 + lh, x * PITCH : x * PITCH + BLOCK, :] for x in range(length)], axis=0
                )
                for lh in range(2)
            ],
            axis=1,
        )
        high, low = halves(both)
        return jnp.dot(
            jnp.concatenate([high, low, high], axis=1), table_ref[cls], preferred_element_type=F32
        )

    def finish(work, cls, result):
        for x in range(length):
            for lh in range(2):
                work[cls * 2 + lh, x * PITCH : x * PITCH + BLOCK, :] = result[
                    x * BLOCK : (x + 1) * BLOCK, lh * 128 : (lh + 1) * 128
                ]

    def sweep(work, chains):
        def rows(x):
            return slice(x * PITCH, x * PITCH + BLOCK)

        def factor(ch, x):
            return jnp.broadcast_to(fac_ref[ch, x : x + 1, :], (BLOCK, 128))

        low, high = {}, {}
        for x in range(half):
            far = length - 1 - x
            for ch in chains:
                scale = factor(ch, x)
                from_low, from_high = work[ch, rows(x), :], work[ch, rows(far), :]
                if x > 0:
                    from_low, from_high = from_low + low[ch], from_high + high[ch]
                low[ch], high[ch] = from_low * scale, from_high * scale
                if x < half - 1:
                    work[ch, rows(x), :] = low[ch]
                    work[ch, rows(far), :] = high[ch]
        for ch in chains:
            scale, meet = factor(ch, half - 1), factor(ch, half)
            low[ch], high[ch] = (low[ch] + scale * high[ch]) * meet, (high[ch] + scale * low[ch]) * meet
            work[ch, rows(half - 1), :] = low[ch]
            work[ch, rows(half), :] = high[ch]
        for x in range(half - 2, -1, -1):
            far = length - 1 - x
            for ch in chains:
                scale = factor(ch, x)
                low[ch] = work[ch, rows(x), :] + scale * low[ch]
                high[ch] = work[ch, rows(far), :] + scale * high[ch]
                work[ch, rows(x), :] = low[ch]
                work[ch, rows(far), :] = high[ch]

    def half_step(work, other, before, after):
        share = BLOCK // 4
        for cls in range(4):
            result = begin(work, cls, fwd_ref)
            for t in range(cls * share, (cls + 1) * share):
                gather(other, before * BLOCK + t, t)
            if cls == 2:
                sweep(work, range(4))
            finish(work, cls, result)
        for cls in range(4):
            result = begin(work, cls, bwd_ref)
            if cls == 0:
                sweep(work, range(4, 8))
            for t in range(cls * share, (cls + 1) * share):
                multiply(other, after * BLOCK + t, t)
            finish(work, cls, result)

    for t in range(BLOCK):
        multiply(even_work, t, t)
    for table in tables:
        table.wait()

    def run_pair(step, carry):
        half_step(even_work, odd_work, 2 * step - 1, 2 * step + 1)
        half_step(odd_work, even_work, 2 * step, 2 * step + 2)
        return carry

    pairs = (live_count + 2 * BLOCK - 1) // (2 * BLOCK)
    lax.fori_loop(0, pairs, run_pair, 0)
    for t in range(BLOCK):
        gather(odd_work, (2 * pairs - 1) * BLOCK + t, t)

    def send_out(owner, carry):
        @pl.when(used[owner] == 0)
        def _():
            out_ref[owner] = jnp.zeros(out_ref.shape[1:], jnp.int16)

        @pl.when(used[owner] > 0)
        def _():
            top = jnp.abs(totals[owner * 8])
            for k in range(1, 8):
                top = jnp.maximum(top, jnp.abs(totals[owner * 8 + k]))
            top = jnp.maximum(jnp.max(top, axis=0, keepdims=True), 2.0**-110)
            power = jnp.ceil(jnp.log2(top) + 1e-4)
            gain = jnp.exp2(-power) * LEVELS
            for k in range(8):
                level = jnp.round(totals[owner * 8 + k] * gain).astype(jnp.int32).astype(jnp.int16)
                for lh in range(2):
                    first = (k * 2 + lh) * half
                    out_ref[owner, first : first + half, :] = level[:, lh * 128 : (lh + 1) * 128]
            codes = jnp.concatenate(
                [jnp.broadcast_to(power[:, lh * 128 : (lh + 1) * 128], (8, 128)) for lh in range(2)], axis=0
            )
            out_ref[owner, 16 * half :, :] = codes.astype(jnp.int32).astype(jnp.int16)

        return carry

    lax.fori_loop(0, nodes, send_out, 0)


def final_kernel(asked_ref, in_ref, code_ref, table_ref, out_ref, totals, work):
    nodes = in_ref.shape[0]
    orbs, width = out_ref.shape
    half = totals.shape[1] // orbs
    plane = width // half
    pitch = half + 1
    totals[...] = jnp.zeros_like(totals)

    def add_one(node, carry):
        target = asked_ref[node, 0, 0]

        @pl.when(target >= 0)
        def _():
            codes = code_ref[node].astype(jnp.int32).astype(F32)
            start = pl.multiple_of(target * half, half)
            for lh in range(2):
                gain = jnp.exp2(codes[lh * 8 : lh * 8 + 1]) * (1.0 / LEVELS)
                for pos in range(4):
                    first = (pos * 2 + lh) * half
                    level = in_ref[node, first : first + half, :].astype(jnp.int32).astype(F32)
                    totals[pos * 2 + lh, pl.ds(start, half), :] += level * gain

        return carry

    lax.fori_loop(0, nodes, add_one, 0)
    for py in range(2):
        rows = jnp.concatenate([totals[py * 4 + j] for j in range(4)], axis=1)
        high, low = halves(rows)
        result = jnp.dot(high, table_ref[py], preferred_element_type=F32) + jnp.dot(
            low, table_ref[py], preferred_element_type=F32
        )
        for j in range(4):
            for orb in range(orbs):
                work[py * 4 + j, orb * pitch : orb * pitch + half, :] = result[
                    orb * half : (orb + 1) * half, j * 128 : (j + 1) * 128
                ]
    for x in range(half):
        for j in range(plane // 128):
            out_ref[:, x * plane + j * 128 : x * plane + (j + 1) * 128] = work[
                j, pl.ds(x, orbs, stride=pitch), :
            ]


def call_solve(orbs, fetch, offsets, pairs, count, incoming):
    nodes, length, plane = incoming.shape
    half = length // 2
    area = half * half
    tables = host_tables(length)
    smem = pl.BlockSpec(memory_space=pltpu.SMEM)
    hbm = pl.BlockSpec(memory_space=pl.ANY)
    work = pltpu.VMEM((8, length * PITCH, 128), F32)
    steps = (pairs.shape[0] // 2 + 2 * BLOCK - 1) // (2 * BLOCK)
    return pl.pallas_call(
        functools.partial(solve_kernel, orbs),
        out_shape=jax.ShapeDtypeStruct((nodes, 16 * half + 16, 128), jnp.int16),
        in_specs=[smem] * 4 + [pl.BlockSpec(memory_space=pltpu.VMEM)] * 2 + [hbm] * 2,
        out_specs=pl.BlockSpec(memory_space=pltpu.VMEM),
        scratch_shapes=[
            pltpu.VMEM((nodes * 32 + 1, half, area), BF16),
            work,
            work,
            pltpu.VMEM((nodes * 8, half, area), F32),
            pltpu.SMEM(((2 * steps + 2) * BLOCK * 9,), jnp.int32),
            pltpu.SMEM((nodes,), jnp.int32),
            pltpu.VMEM((4, 3 * area, area), BF16),
            pltpu.VMEM((4, 3 * area, area), BF16),
            pltpu.VMEM((8, half + 8, 128), F32),
            pltpu.SemaphoreType.DMA((7,)),
        ],
        compiler_params=pltpu.CompilerParams(vmem_limit_bytes=(10 << 20) + nodes * (704 << 10)),
        name="solve",
    )(
        fetch, offsets, pairs, count, incoming,
        tables["variants"], tables["sines"], tables["factors"],
    )


def on_device(phi, offsets, fetch, task_pairs, task_count):
    nodes = lax.axis_size("orb")
    orbs, volume = phi.shape
    length = cube_root(volume)
    half, plane = length // 2, length * length
    tables = host_tables(length)
    smem = pl.BlockSpec(memory_space=pltpu.SMEM)
    vmem = pl.BlockSpec(memory_space=pltpu.VMEM)
    params = pltpu.CompilerParams(vmem_limit_bytes=(12 << 20) + nodes * (384 << 10))
    fetch = fetch.reshape(-1)
    asking = pl.pallas_call(
        ask_kernel,
        out_shape=jax.ShapeDtypeStruct((nodes, 1, 128), jnp.int32),
        in_specs=[smem],
        out_specs=vmem,
        name="ask",
    )(fetch)
    packed = pl.pallas_call(
        pack_kernel,
        out_shape=jax.ShapeDtypeStruct((orbs, length, plane), BF16),
        in_specs=[vmem, vmem],
        out_specs=vmem,
        scratch_shapes=[pltpu.VMEM((plane // 128, (orbs + 1) * length, 128), F32)],
        compiler_params=params,
        name="pack",
    )(phi, tables["pack"])
    asked = lax.all_to_all(asking, "orb", split_axis=0, concat_axis=0, tiled=True)
    outgoing = pl.pallas_call(
        pick_kernel,
        out_shape=jax.ShapeDtypeStruct((nodes, length, plane), BF16),
        in_specs=[smem, vmem],
        out_specs=pl.BlockSpec(memory_space=pl.ANY),
        scratch_shapes=[pltpu.SemaphoreType.DMA((nodes,))],
        compiler_params=params,
        name="pick",
    )(asked, packed)
    incoming = lax.all_to_all(outgoing, "orb", split_axis=0, concat_axis=0, tiled=True)
    partial = call_solve(
        orbs, fetch, offsets.reshape(-1), task_pairs.reshape(-1), task_count, incoming
    )
    returned = lax.all_to_all(partial, "orb", split_axis=0, concat_axis=0, tiled=True)
    return pl.pallas_call(
        final_kernel,
        grid=(2,),
        out_shape=jax.ShapeDtypeStruct((orbs, volume), F32),
        in_specs=[
            smem,
            pl.BlockSpec((nodes, 8 * half, 128), lambda hx: (0, hx, 0)),
            pl.BlockSpec((nodes, 16, 128), lambda hx: (0, half, 0)),
            pl.BlockSpec((2, plane // 2, plane // 2), lambda hx: (0, 0, 0)),
        ],
        out_specs=pl.BlockSpec((orbs, volume // 2), lambda hx: (0, hx)),
        scratch_shapes=[
            pltpu.VMEM((8, orbs * half, 128), F32),
            pltpu.VMEM((plane // 128, orbs * (half + 1), 128), F32),
        ],
        compiler_params=params,
        name="final",
    )(asked, returned, returned, tables["unpack"])


def solution(mesh):
    in_specs = (
        P(("groups", "orb"), None),
        P("groups", None),
        P(("groups", "orb"), None),
        P(("groups", "orb"), None),
        P(("groups", "orb")),
    )
    out_specs = P(("groups", "orb"), None)
    return jax.shard_map(
        on_device, mesh=mesh, in_specs=in_specs, out_specs=out_specs, check_vma=False
    )
```

```python
import functools

import jax
import jax.numpy as jnp
import ml_dtypes
import numpy as np
from jax import lax
from jax.experimental import pallas as pl
from jax.experimental.pallas import tpu as pltpu
from jax.sharding import PartitionSpec as P

BLOCK = 8
PITCH = 9
LEVELS = 32704.0
BF16 = jnp.bfloat16
F32 = jnp.float32


def cube_root(volume):
    length = 1
    while length * length * length < volume:
        length = length + 1
    return length


def split_bf16(values):
    high = values.astype(ml_dtypes.bfloat16)
    low = (values - high.astype(np.float64)).astype(ml_dtypes.bfloat16)
    return high, low


def host_tables(length):
    half = length // 2
    area = half * half
    count = np.arange(length) + 1.0
    eigen = 2.0 - 2.0 * np.cos(np.pi * count / (length + 1))
    modes = [eigen[0::2][::-1], eigen[1::2]]
    near = np.arange(half) + 1.0
    sine = np.sqrt(2.0 / (length + 1)) * np.sin(2.0 * np.pi * np.outer(near, near) / (length + 1))
    high, low = split_bf16(np.kron(sine, sine))
    sines = np.concatenate([high, high, low], axis=0)
    factors = []
    for par_y in (0, 1):
        for par_z in (0, 1):
            beta = 2.0 + (modes[par_y][:, None] + modes[par_z][None, :]).reshape(area)
            rows = [1.0 / beta]
            for _ in range(half - 1):
                rows.append(1.0 / (beta - rows[-1]))
            rows.append(1.0 / (1.0 - rows[-1] ** 2))
            rows.extend([rows[-1]] * 7)
            rows = np.stack(rows).astype(np.float32)
            factors.append(rows)
    place = np.arange(area)
    low_y, low_z = place // half, place % half
    variants = []
    for rev_y, rev_z in ((0, 1), (1, 0), (1, 1)):
        src_y = half - 1 - low_y if rev_y else low_y
        src_z = half - 1 - low_z if rev_z else low_z
        one_hot = np.zeros((area, area), ml_dtypes.bfloat16)
        one_hot[src_y * half + src_z, place] = 1
        variants.append(one_hot)
    wide = 2 * area
    spot = np.arange(wide)
    pack = np.zeros((wide, wide), ml_dtypes.bfloat16)
    z_half, rest = spot // area, spot % area
    pack[(rest // half) * length + z_half * half + rest % half, spot] = 1
    spot = np.arange(area)
    z_half, rest = spot // (area // 2), spot % (area // 2)
    unpack = []
    for par_y in (0, 1):
        y_nat = half // 2 - 1 - rest // half if par_y else rest // half
        z_nat = np.where(z_half == 1, length - 1 - rest % half, rest % half)
        one_hot = np.zeros((area, area), ml_dtypes.bfloat16)
        one_hot[spot, y_nat * length + z_nat] = 1
        unpack.append(one_hot)
    left = np.concatenate(factors).astype(np.float64)
    pieces = []
    for _ in range(3):
        pieces.append(left.astype(ml_dtypes.bfloat16))
        left = left - pieces[-1].astype(np.float64)
    variants = np.concatenate(
        [np.concatenate(variants, axis=1), np.concatenate(pieces, axis=1)], axis=0
    )
    return dict(sines=sines, variants=variants, pack=pack, unpack=np.stack(unpack))


def halves(value):
    high = value.astype(BF16)
    low = (value - high.astype(F32)).astype(BF16)
    return high, low


def ask_kernel(fetch_ref, out_ref):
    for node in range(out_ref.shape[0]):
        out_ref[node] = jnp.full(out_ref.shape[1:], fetch_ref[node], jnp.int32)


def pack_kernel(phi_ref, table_ref, out_ref, work):
    orbs = phi_ref.shape[0]
    length = out_ref.shape[1]
    plane = length * length
    wide = plane // 2
    pitch = orbs + 1
    for y_half in range(2):
        rows = jnp.concatenate(
            [phi_ref[:, x * plane + y_half * wide : x * plane + (y_half + 1) * wide] for x in range(length)],
            axis=0,
        )
        moved = jnp.dot(rows, table_ref[...], preferred_element_type=F32)
        for j in range(wide // 128):
            for x in range(length):
                work[y_half * (wide // 128) + j, x * pitch : x * pitch + orbs, :] = moved[
                    x * orbs : (x + 1) * orbs, j * 128 : (j + 1) * 128
                ]
    for orb in range(orbs):
        for j in range(plane // 128):
            piece = work[j, pl.ds(orb, length, stride=pitch), :]
            out_ref[orb, :, j * 128 : (j + 1) * 128] = piece.astype(BF16)


def pick_kernel(asked_ref, packed_ref, out_ref, sems):
    copies = []
    for node in range(out_ref.shape[0]):
        orb = jnp.maximum(asked_ref[node, 0, 0], 0)
        copies.append(pltpu.make_async_copy(packed_ref.at[orb], out_ref.at[node], sems.at[node]))
        copies[-1].start()
    for copy in copies:
        copy.wait()


def solve_kernel(
    orbs, slots, ints_ref, in_ref, var_ref, sine_hbm,
    out_ref, octs, even_work, odd_work, totals, plan, used, sine_ref, fac_ref, signs, sem,
):
    nodes, length = in_ref.shape[0], in_ref.shape[1]
    half = length // 2
    area = half * half
    zero_at = nodes * 32
    group = 8
    table = pltpu.make_async_copy(sine_hbm, sine_ref, sem)
    table.start()
    row_at = lax.broadcasted_iota(jnp.int32, (half, area), 1)
    turn_z = 1.0 - 2.0 * (row_at % 2).astype(F32)
    turn_y = 1.0 - 2.0 * (row_at // half % 2).astype(F32)
    signs[0] = turn_y * turn_z
    signs[1] = turn_y
    signs[2] = turn_z
    octs[zero_at] = jnp.zeros((half, area), BF16)
    fetch_at, offset_at, pair_at = 1, 1 + nodes, 1 + nodes + nodes * orbs * 3
    live_count = ints_ref[0]
    last_slot = slots - 1

    def make_variants(step, carry):
        for quad in range(4):
            block = in_ref[pl.ds(step * group, group), :, quad * area : (quad + 1) * area]
            turned = jnp.dot(
                block.reshape(group * length, area), var_ref[:area, :], preferred_element_type=F32
            ).astype(BF16)
            for one in range(group):
                for hx in range(2):
                    base = (((step * group + one) * 2 + hx) * 4 + quad) * 4
                    octs[base] = block[one, hx * half : (hx + 1) * half]
                    first = one * length + hx * half
                    for rev in range(3):
                        octs[base + 1 + rev] = turned[first : first + half, rev * area : (rev + 1) * area]
        return carry

    lax.fori_loop(0, nodes // group, make_variants, 0)

    def clear(step, carry):
        for k in range(8):
            totals[step * 8 + k] = jnp.zeros((half, area), F32)
        used[step] = 0
        return carry

    lax.fori_loop(0, nodes, clear, 0)
    for ch in range(8):
        even_work[ch] = jnp.zeros(even_work.shape[1:], F32)
        odd_work[ch] = jnp.zeros(odd_work.shape[1:], F32)
    for t in range(BLOCK):
        plan[t * 9] = 0
        for k in range(8):
            plan[t * 9 + 1 + k] = zero_at

    def multiply(work, slot, t):
        at = jnp.minimum(slot, last_slot)
        first, second = ints_ref[pair_at + 2 * at], ints_ref[pair_at + 2 * at + 1]
        id_a = first * orbs + jnp.maximum(ints_ref[fetch_at + first], 0)
        id_b = second * orbs + jnp.maximum(ints_ref[fetch_at + second], 0)
        shift = [ints_ref[offset_at + id_a * 3 + k] - ints_ref[offset_at + id_b * 3 + k] for k in range(3)]
        fits = [[(side + shift[k] >= 0) & (side + shift[k] < 2) for side in range(2)] for k in range(3)]
        start = second * 32 + shift[0] * 16 + shift[1] * 8 + shift[2] * 4
        live = slot < live_count
        note = (slot + BLOCK) * 9
        plan[note] = first
        used[first] = jnp.where(live, 1, used[first])
        for hx in range(2):
            dens = []
            for pos in range(4):
                py, pz = pos // 2, pos % 2
                inside = live & fits[0][hx] & fits[1][py] & fits[2][pz]
                spot = jnp.where(inside, start + (hx * 16 + py * 8 + pz * 4 + pos), zero_at)
                plan[note + 1 + hx * 4 + pos] = spot
                own = octs[first * 32 + (hx * 16 + pos * 5)].astype(F32)
                dens.append(own * octs[spot].astype(F32))
            even0, odd0 = dens[0] + dens[1], dens[0] - dens[1]
            even1, odd1 = dens[2] + dens[3], dens[2] - dens[3]
            folded = (
                (even0 + even1) * signs[0],
                (odd0 + odd1) * signs[1],
                (even0 - even1) * signs[2],
                odd0 - odd1,
            )
            for cls in range(4):
                for lh in range(2):
                    work[cls * 2 + lh, pl.ds(hx * half * PITCH + t, half, stride=PITCH), :] = folded[cls][
                        :, lh * 128 : (lh + 1) * 128
                    ]

    def gather(work, slot, t):
        note = (slot + BLOCK) * 9
        first = plan[note] * 8
        for hx in range(2):
            folded = []
            for cls in range(4):
                pieces = [
                    work[cls * 2 + lh, pl.ds(hx * half * PITCH + t, half, stride=PITCH), :] for lh in range(2)
                ]
                piece = jnp.concatenate(pieces, axis=1)
                folded.append(piece * signs[cls] if cls < 3 else piece)
            sum0, dif0 = folded[0] + folded[1], folded[0] - folded[1]
            sum1, dif1 = folded[2] + folded[3], folded[2] - folded[3]
            potential = (sum0 + sum1, dif0 + dif1, sum0 - sum1, dif0 - dif1)
            for pos in range(4):
                moved = octs[plan[note + 1 + hx * 4 + pos]].astype(F32)
                totals[first + (hx * 4 + pos)] += potential[pos] * moved

    def begin(work, cls):
        both = jnp.concatenate(
            [
                jnp.concatenate(
                    [work[cls * 2 + lh, x * PITCH : x * PITCH + BLOCK, :] for x in range(length)], axis=0
                )
                for lh in range(2)
            ],
            axis=1,
        )
        high, low = halves(both)
        return jnp.dot(
            jnp.concatenate([high, low, high], axis=1), sine_ref[...], preferred_element_type=F32
        )

    def finish(work, cls, result):
        for x in range(length):
            for lh in range(2):
                work[cls * 2 + lh, x * PITCH : x * PITCH + BLOCK, :] = result[
                    x * BLOCK : (x + 1) * BLOCK, lh * 128 : (lh + 1) * 128
                ]

    def sweep(work, chains):
        def rows(x):
            return slice(x * PITCH, x * PITCH + BLOCK)

        def factor(ch, x):
            return jnp.broadcast_to(fac_ref[ch, x : x + 1, :], (BLOCK, 128))

        low, high = {}, {}
        for x in range(half):
            far = length - 1 - x
            for ch in chains:
                scale = factor(ch, x)
                from_low, from_high = work[ch, rows(x), :], work[ch, rows(far), :]
                if x > 0:
                    from_low, from_high = from_low + low[ch], from_high + high[ch]
                low[ch], high[ch] = from_low * scale, from_high * scale
                if x < half - 1:
                    work[ch, rows(x), :] = low[ch]
                    work[ch, rows(far), :] = high[ch]
        for ch in chains:
            scale, meet = factor(ch, half - 1), factor(ch, half)
            low[ch], high[ch] = (low[ch] + scale * high[ch]) * meet, (high[ch] + scale * low[ch]) * meet
            work[ch, rows(half - 1), :] = low[ch]
            work[ch, rows(half), :] = high[ch]
        for x in range(half - 2, -1, -1):
            far = length - 1 - x
            for ch in chains:
                scale = factor(ch, x)
                low[ch] = work[ch, rows(x), :] + scale * low[ch]
                high[ch] = work[ch, rows(far), :] + scale * high[ch]
                work[ch, rows(x), :] = low[ch]
                work[ch, rows(far), :] = high[ch]

    def half_step(work, other, before, after):
        share = BLOCK // 4
        for cls in range(4):
            result = begin(work, cls)
            for t in range(cls * share, (cls + 1) * share):
                gather(other, before * BLOCK + t, t)
            if cls == 2:
                sweep(work, range(4))
            finish(work, cls, result)
        for cls in range(4):
            result = begin(work, cls)
            if cls == 0:
                sweep(work, range(4, 8))
            for t in range(cls * share, (cls + 1) * share):
                multiply(other, after * BLOCK + t, t)
            finish(work, cls, result)

    for t in range(BLOCK):
        multiply(even_work, t, t)
    table.wait()
    steps = fac_ref.shape[1]
    terms = [var_ref[area:, k * area : (k + 1) * area].astype(F32) for k in range(3)]
    joined = (terms[2] + terms[1]) + terms[0]
    for ch in range(8):
        first, lanes = ch // 2 * steps, ch % 2 * 128
        fac_ref[ch] = joined[first : first + steps, lanes : lanes + 128]

    def run_pair(step, carry):
        half_step(even_work, odd_work, 2 * step - 1, 2 * step + 1)
        half_step(odd_work, even_work, 2 * step, 2 * step + 2)
        return carry

    pairs = (live_count + 2 * BLOCK - 1) // (2 * BLOCK)
    lax.fori_loop(0, pairs, run_pair, 0)
    for t in range(BLOCK):
        gather(odd_work, (2 * pairs - 1) * BLOCK + t, t)

    def send_out(owner, carry):
        @pl.when(used[owner] == 0)
        def _():
            out_ref[owner] = jnp.zeros(out_ref.shape[1:], jnp.int16)

        @pl.when(used[owner] > 0)
        def _():
            top = jnp.abs(totals[owner * 8])
            for k in range(1, 8):
                top = jnp.maximum(top, jnp.abs(totals[owner * 8 + k]))
            top = jnp.maximum(jnp.max(top, axis=0, keepdims=True), 2.0**-110)
            power = jnp.ceil(jnp.log2(top) + 1e-4)
            gain = jnp.exp2(-power) * LEVELS
            for k in range(8):
                level = jnp.round(totals[owner * 8 + k] * gain).astype(jnp.int32).astype(jnp.int16)
                for lh in range(2):
                    first = (k * 2 + lh) * half
                    out_ref[owner, first : first + half, :] = level[:, lh * 128 : (lh + 1) * 128]
            codes = jnp.concatenate(
                [jnp.broadcast_to(power[:, lh * 128 : (lh + 1) * 128], (8, 128)) for lh in range(2)], axis=0
            )
            out_ref[owner, 16 * half :, :] = codes.astype(jnp.int32).astype(jnp.int16)

        return carry

    lax.fori_loop(0, nodes, send_out, 0)


def final_kernel(asked_ref, in_ref, code_ref, table_ref, out_ref, totals, work):
    nodes = in_ref.shape[0]
    orbs, width = out_ref.shape
    half = totals.shape[1] // orbs
    plane = width // half
    pitch = half + 1
    totals[...] = jnp.zeros_like(totals)

    def add_one(node, carry):
        target = asked_ref[node, 0, 0]

        @pl.when(target >= 0)
        def _():
            codes = code_ref[node].astype(jnp.int32).astype(F32)
            start = pl.multiple_of(target * half, half)
            for lh in range(2):
                gain = jnp.exp2(codes[lh * 8 : lh * 8 + 1]) * (1.0 / LEVELS)
                for pos in range(4):
                    first = (pos * 2 + lh) * half
                    level = in_ref[node, first : first + half, :].astype(jnp.int32).astype(F32)
                    totals[pos * 2 + lh, pl.ds(start, half), :] += level * gain

        return carry

    lax.fori_loop(0, nodes, add_one, 0)
    for py in range(2):
        for m in range(2):
            rows = jnp.concatenate([totals[py * 4 + m], totals[py * 4 + 2 + m]], axis=1)
            high, low = halves(rows)
            result = jnp.dot(high, table_ref[py], preferred_element_type=F32) + jnp.dot(
                low, table_ref[py], preferred_element_type=F32
            )
            first = py * 4 + 2 * (1 - m if py else m)
            for j in range(2):
                for orb in range(orbs):
                    work[first + j, orb * pitch : orb * pitch + half, :] = result[
                        orb * half : (orb + 1) * half, j * 128 : (j + 1) * 128
                    ]
    for x in range(half):
        for j in range(plane // 128):
            out_ref[:, x * plane + j * 128 : x * plane + (j + 1) * 128] = work[
                j, pl.ds(x, orbs, stride=pitch), :
            ]


def call_solve(orbs, fetch, offsets, pairs, count, incoming):
    nodes, length, plane = incoming.shape
    half = length // 2
    area = half * half
    tables = host_tables(length)
    smem = pl.BlockSpec(memory_space=pltpu.SMEM)
    hbm = pl.BlockSpec(memory_space=pl.ANY)
    work = pltpu.VMEM((8, length * PITCH, 128), F32)
    steps = (pairs.shape[0] // 2 + 2 * BLOCK - 1) // (2 * BLOCK)
    return pl.pallas_call(
        functools.partial(solve_kernel, orbs, pairs.shape[0] // 2),
        out_shape=jax.ShapeDtypeStruct((nodes, 16 * half + 16, 128), jnp.int16),
        in_specs=[smem] + [pl.BlockSpec(memory_space=pltpu.VMEM)] * 2 + [hbm],
        out_specs=pl.BlockSpec(memory_space=pltpu.VMEM),
        scratch_shapes=[
            pltpu.VMEM((nodes * 32 + 1, half, area), BF16),
            work,
            work,
            pltpu.VMEM((nodes * 8, half, area), F32),
            pltpu.SMEM(((2 * steps + 2) * BLOCK * 9,), jnp.int32),
            pltpu.SMEM((nodes,), jnp.int32),
            pltpu.VMEM((3 * area, area), BF16),
            pltpu.VMEM((8, half + 8, 128), F32),
            pltpu.VMEM((3, half, area), F32),
            pltpu.SemaphoreType.DMA,
        ],
        compiler_params=pltpu.CompilerParams(vmem_limit_bytes=(10 << 20) + nodes * (704 << 10)),
        name="solve",
    )(
        jnp.concatenate([count, fetch, offsets, pairs]), incoming, tables["variants"], tables["sines"]
    )


def on_device(phi, offsets, fetch, task_pairs, task_count):
    nodes = lax.axis_size("orb")
    orbs, volume = phi.shape
    length = cube_root(volume)
    half, plane = length // 2, length * length
    tables = host_tables(length)
    smem = pl.BlockSpec(memory_space=pltpu.SMEM)
    vmem = pl.BlockSpec(memory_space=pltpu.VMEM)
    params = pltpu.CompilerParams(vmem_limit_bytes=(12 << 20) + nodes * (384 << 10))
    fetch = fetch.reshape(-1)
    asking = pl.pallas_call(
        ask_kernel,
        out_shape=jax.ShapeDtypeStruct((nodes, 1, 128), jnp.int32),
        in_specs=[smem],
        out_specs=vmem,
        name="ask",
    )(fetch)
    packed = pl.pallas_call(
        pack_kernel,
        out_shape=jax.ShapeDtypeStruct((orbs, length, plane), BF16),
        in_specs=[vmem, vmem],
        out_specs=vmem,
        scratch_shapes=[pltpu.VMEM((plane // 128, (orbs + 1) * length, 128), F32)],
        compiler_params=params,
        name="pack",
    )(phi, tables["pack"])
    asked = lax.all_to_all(asking, "orb", split_axis=0, concat_axis=0, tiled=True)
    outgoing = pl.pallas_call(
        pick_kernel,
        out_shape=jax.ShapeDtypeStruct((nodes, length, plane), BF16),
        in_specs=[smem, vmem],
        out_specs=pl.BlockSpec(memory_space=pl.ANY),
        scratch_shapes=[pltpu.SemaphoreType.DMA((nodes,))],
        compiler_params=params,
        name="pick",
    )(asked, packed)
    incoming = lax.all_to_all(outgoing, "orb", split_axis=0, concat_axis=0, tiled=True)
    partial = call_solve(
        orbs, fetch, offsets.reshape(-1), task_pairs.reshape(-1), task_count, incoming
    )
    returned = lax.all_to_all(partial, "orb", split_axis=0, concat_axis=0, tiled=True)
    return pl.pallas_call(
        final_kernel,
        grid=(2,),
        out_shape=jax.ShapeDtypeStruct((orbs, volume), F32),
        in_specs=[
            smem,
            pl.BlockSpec((nodes, 8 * half, 128), lambda hx: (0, hx, 0)),
            pl.BlockSpec((nodes, 16, 128), lambda hx: (0, half, 0)),
            pl.BlockSpec((2, plane // 4, plane // 4), lambda hx: (0, 0, 0)),
        ],
        out_specs=pl.BlockSpec((orbs, volume // 2), lambda hx: (0, hx)),
        scratch_shapes=[
            pltpu.VMEM((8, orbs * half, 128), F32),
            pltpu.VMEM((plane // 128, orbs * (half + 1), 128), F32),
        ],
        compiler_params=params,
        name="final",
    )(asked, returned, returned, tables["unpack"])


def solution(mesh):
    in_specs = (
        P(("groups", "orb"), None),
        P("groups", None),
        P(("groups", "orb"), None),
        P(("groups", "orb"), None),
        P(("groups", "orb")),
    )
    out_specs = P(("groups", "orb"), None)
    return jax.shard_map(
        on_device, mesh=mesh, in_specs=in_specs, out_specs=out_specs, check_vma=False
    )
```

```python
import functools

import jax
import jax.numpy as jnp
import ml_dtypes
import numpy as np
from jax import lax
from jax.experimental import pallas as pl
from jax.experimental.pallas import tpu as pltpu
from jax.sharding import PartitionSpec as P

BLOCK = 8
PITCH = 9
LEVELS = 32704.0
BF16 = jnp.bfloat16
F32 = jnp.float32


def cube_root(volume):
    length = 1
    while length * length * length < volume:
        length = length + 1
    return length


def split_bf16(values):
    high = values.astype(ml_dtypes.bfloat16)
    low = (values - high.astype(np.float64)).astype(ml_dtypes.bfloat16)
    return high, low


def host_tables(length):
    half = length // 2
    area = half * half
    count = np.arange(length) + 1.0
    eigen = 2.0 - 2.0 * np.cos(np.pi * count / (length + 1))
    modes = [eigen[0::2][::-1], eigen[1::2]]
    near = np.arange(half) + 1.0
    sine = np.sqrt(2.0 / (length + 1)) * np.sin(2.0 * np.pi * np.outer(near, near) / (length + 1))
    high, low = split_bf16(np.kron(sine, sine))
    sines = np.concatenate([high, high, low], axis=0)
    factors = []
    for par_y in (0, 1):
        for par_z in (0, 1):
            beta = 2.0 + (modes[par_y][:, None] + modes[par_z][None, :]).reshape(area)
            rows = [1.0 / beta]
            for _ in range(half - 1):
                rows.append(1.0 / (beta - rows[-1]))
            rows.append(1.0 / (1.0 - rows[-1] ** 2))
            rows.extend([rows[-1]] * 7)
            rows = np.stack(rows).astype(np.float32)
            factors.append(rows)
    place = np.arange(area)
    low_y, low_z = place // half, place % half
    variants = []
    for rev_y, rev_z in ((0, 1), (1, 0), (1, 1)):
        src_y = half - 1 - low_y if rev_y else low_y
        src_z = half - 1 - low_z if rev_z else low_z
        one_hot = np.zeros((area, area), ml_dtypes.bfloat16)
        one_hot[src_y * half + src_z, place] = 1
        variants.append(one_hot)
    wide = 2 * area
    spot = np.arange(wide)
    pack = np.zeros((wide, wide), ml_dtypes.bfloat16)
    z_half, rest = spot // area, spot % area
    pack[(rest // half) * length + z_half * half + rest % half, spot] = 1
    spot = np.arange(area)
    z_half, rest = spot // (area // 2), spot % (area // 2)
    unpack = []
    for par_y in (0, 1):
        y_nat = half // 2 - 1 - rest // half if par_y else rest // half
        z_nat = np.where(z_half == 1, length - 1 - rest % half, rest % half)
        one_hot = np.zeros((area, area), ml_dtypes.bfloat16)
        one_hot[spot, y_nat * length + z_nat] = 1
        unpack.append(one_hot)
    left = np.concatenate(factors).astype(np.float64)
    pieces = []
    for _ in range(3):
        pieces.append(left.astype(ml_dtypes.bfloat16))
        left = left - pieces[-1].astype(np.float64)
    variants = np.concatenate(
        [np.concatenate(variants, axis=1), np.concatenate(pieces, axis=1)], axis=0
    )
    return dict(sines=sines, variants=variants, pack=pack, unpack=np.stack(unpack))


def halves(value):
    high = value.astype(BF16)
    low = (value - high.astype(F32)).astype(BF16)
    return high, low


def ask_kernel(fetch_ref, out_ref):
    for node in range(out_ref.shape[0]):
        out_ref[node] = jnp.full(out_ref.shape[1:], fetch_ref[node], jnp.int32)


def pack_kernel(phi_ref, table_ref, out_ref, work):
    orbs = phi_ref.shape[0]
    length = out_ref.shape[1]
    plane = length * length
    wide = plane // 2
    pitch = orbs + 1
    for y_half in range(2):
        rows = jnp.concatenate(
            [phi_ref[:, x * plane + y_half * wide : x * plane + (y_half + 1) * wide] for x in range(length)],
            axis=0,
        )
        moved = jnp.dot(rows, table_ref[...], preferred_element_type=F32)
        for j in range(wide // 128):
            for x in range(length):
                work[y_half * (wide // 128) + j, x * pitch : x * pitch + orbs, :] = moved[
                    x * orbs : (x + 1) * orbs, j * 128 : (j + 1) * 128
                ]
    for orb in range(orbs):
        for j in range(plane // 128):
            piece = work[j, pl.ds(orb, length, stride=pitch), :]
            out_ref[orb, :, j * 128 : (j + 1) * 128] = piece.astype(BF16)


def pick_kernel(asked_ref, packed_ref, out_ref, sems):
    copies = []
    for node in range(out_ref.shape[0]):
        orb = jnp.maximum(asked_ref[node, 0, 0], 0)
        copies.append(pltpu.make_async_copy(packed_ref.at[orb], out_ref.at[node], sems.at[node]))
        copies[-1].start()
    for copy in copies:
        copy.wait()


def solve_kernel(
    orbs, slots, ints_ref, in_ref, var_ref, sine_hbm,
    out_ref, octs, work, totals, plan, used, sine_ref, fac_ref, signs, sem,
):
    nodes, length = in_ref.shape[0], in_ref.shape[1]
    half = length // 2
    area = half * half
    zero_at = nodes * 32
    group = 8
    table = pltpu.make_async_copy(sine_hbm, sine_ref, sem)
    table.start()
    row_at = lax.broadcasted_iota(jnp.int32, (half, area), 1)
    turn_z = 1.0 - 2.0 * (row_at % 2).astype(F32)
    turn_y = 1.0 - 2.0 * (row_at // half % 2).astype(F32)
    signs[0] = turn_y * turn_z
    signs[1] = turn_y
    signs[2] = turn_z
    octs[zero_at] = jnp.zeros((half, area), BF16)
    fetch_at, offset_at, pair_at = 1, 1 + nodes, 1 + nodes + nodes * orbs * 3
    live_count = ints_ref[0]
    last_slot = slots - 1

    def make_variants(step, carry):
        for quad in range(4):
            block = in_ref[pl.ds(step * group, group), :, quad * area : (quad + 1) * area]
            turned = jnp.dot(
                block.reshape(group * length, area), var_ref[:area, :], preferred_element_type=F32
            ).astype(BF16)
            for one in range(group):
                for hx in range(2):
                    base = (((step * group + one) * 2 + hx) * 4 + quad) * 4
                    octs[base] = block[one, hx * half : (hx + 1) * half]
                    first = one * length + hx * half
                    for rev in range(3):
                        octs[base + 1 + rev] = turned[first : first + half, rev * area : (rev + 1) * area]
        return carry

    lax.fori_loop(0, nodes // group, make_variants, 0)

    def clear(step, carry):
        for k in range(8):
            totals[step * 8 + k] = jnp.zeros((half, area), F32)
        used[step] = 0
        return carry

    lax.fori_loop(0, nodes, clear, 0)

    def multiply(work, slot, t):
        at = jnp.minimum(slot, last_slot)
        first, second = ints_ref[pair_at + 2 * at], ints_ref[pair_at + 2 * at + 1]
        id_a = first * orbs + jnp.maximum(ints_ref[fetch_at + first], 0)
        id_b = second * orbs + jnp.maximum(ints_ref[fetch_at + second], 0)
        shift = [ints_ref[offset_at + id_a * 3 + k] - ints_ref[offset_at + id_b * 3 + k] for k in range(3)]
        fits = [[(side + shift[k] >= 0) & (side + shift[k] < 2) for side in range(2)] for k in range(3)]
        start = second * 32 + shift[0] * 16 + shift[1] * 8 + shift[2] * 4
        live = slot < live_count
        note = t * 9
        plan[note] = first
        used[first] = jnp.where(live, 1, used[first])
        for hx in range(2):
            dens = []
            for pos in range(4):
                py, pz = pos // 2, pos % 2
                inside = live & fits[0][hx] & fits[1][py] & fits[2][pz]
                spot = jnp.where(inside, start + (hx * 16 + py * 8 + pz * 4 + pos), zero_at)
                plan[note + 1 + hx * 4 + pos] = spot
                own = octs[first * 32 + (hx * 16 + pos * 5)].astype(F32)
                dens.append(own * octs[spot].astype(F32))
            even0, odd0 = dens[0] + dens[1], dens[0] - dens[1]
            even1, odd1 = dens[2] + dens[3], dens[2] - dens[3]
            folded = (
                (even0 + even1) * signs[0],
                (odd0 + odd1) * signs[1],
                (even0 - even1) * signs[2],
                odd0 - odd1,
            )
            for cls in range(4):
                for lh in range(2):
                    work[cls * 2 + lh, pl.ds(hx * half * PITCH + t, half, stride=PITCH), :] = folded[cls][
                        :, lh * 128 : (lh + 1) * 128
                    ]

    def gather(work, slot, t):
        note = t * 9
        first = plan[note] * 8
        for hx in range(2):
            folded = []
            for cls in range(4):
                pieces = [
                    work[cls * 2 + lh, pl.ds(hx * half * PITCH + t, half, stride=PITCH), :] for lh in range(2)
                ]
                piece = jnp.concatenate(pieces, axis=1)
                folded.append(piece * signs[cls] if cls < 3 else piece)
            sum0, dif0 = folded[0] + folded[1], folded[0] - folded[1]
            sum1, dif1 = folded[2] + folded[3], folded[2] - folded[3]
            potential = (sum0 + sum1, dif0 + dif1, sum0 - sum1, dif0 - dif1)
            for pos in range(4):
                moved = octs[plan[note + 1 + hx * 4 + pos]].astype(F32)
                totals[first + (hx * 4 + pos)] += potential[pos] * moved

    def begin(work, cls):
        both = jnp.concatenate(
            [
                jnp.concatenate(
                    [work[cls * 2 + lh, x * PITCH : x * PITCH + BLOCK, :] for x in range(length)], axis=0
                )
                for lh in range(2)
            ],
            axis=1,
        )
        high, low = halves(both)
        return jnp.dot(
            jnp.concatenate([high, low, high], axis=1), sine_ref[...], preferred_element_type=F32
        )

    def finish(work, cls, result):
        for x in range(length):
            for lh in range(2):
                work[cls * 2 + lh, x * PITCH : x * PITCH + BLOCK, :] = result[
                    x * BLOCK : (x + 1) * BLOCK, lh * 128 : (lh + 1) * 128
                ]

    def sweep(work, chains):
        def rows(x):
            return slice(x * PITCH, x * PITCH + BLOCK)

        def factor(ch, x):
            return jnp.broadcast_to(fac_ref[ch, x : x + 1, :], (BLOCK, 128))

        low, high = {}, {}
        for x in range(half):
            far = length - 1 - x
            for ch in chains:
                scale = factor(ch, x)
                from_low, from_high = work[ch, rows(x), :], work[ch, rows(far), :]
                if x > 0:
                    from_low, from_high = from_low + low[ch], from_high + high[ch]
                low[ch], high[ch] = from_low * scale, from_high * scale
                if x < half - 1:
                    work[ch, rows(x), :] = low[ch]
                    work[ch, rows(far), :] = high[ch]
        for ch in chains:
            scale, meet = factor(ch, half - 1), factor(ch, half)
            low[ch], high[ch] = (low[ch] + scale * high[ch]) * meet, (high[ch] + scale * low[ch]) * meet
            work[ch, rows(half - 1), :] = low[ch]
            work[ch, rows(half), :] = high[ch]
        for x in range(half - 2, -1, -1):
            far = length - 1 - x
            for ch in chains:
                scale = factor(ch, x)
                low[ch] = work[ch, rows(x), :] + scale * low[ch]
                high[ch] = work[ch, rows(far), :] + scale * high[ch]
                work[ch, rows(x), :] = low[ch]
                work[ch, rows(far), :] = high[ch]

    table.wait()
    steps = fac_ref.shape[1]
    terms = [var_ref[area:, k * area : (k + 1) * area].astype(F32) for k in range(3)]
    joined = (terms[2] + terms[1]) + terms[0]
    for ch in range(8):
        first, lanes = ch // 2 * steps, ch % 2 * 128
        fac_ref[ch] = joined[first : first + steps, lanes : lanes + 128]

    def run_block(step, carry):
        for t in range(BLOCK):
            multiply(work, step * BLOCK + t, t)
        for cls in range(4):
            result = begin(work, cls)
            finish(work, cls, result)
        sweep(work, range(8))
        for cls in range(4):
            result = begin(work, cls)
            finish(work, cls, result)
        for t in range(BLOCK):
            gather(work, step * BLOCK + t, t)
        return carry

    lax.fori_loop(0, (live_count + BLOCK - 1) // BLOCK, run_block, 0)

    def send_out(owner, carry):
        @pl.when(used[owner] == 0)
        def _():
            out_ref[owner] = jnp.zeros(out_ref.shape[1:], jnp.int16)

        @pl.when(used[owner] > 0)
        def _():
            top = jnp.abs(totals[owner * 8])
            for k in range(1, 8):
                top = jnp.maximum(top, jnp.abs(totals[owner * 8 + k]))
            top = jnp.maximum(jnp.max(top, axis=0, keepdims=True), 2.0**-110)
            power = jnp.ceil(jnp.log2(top) + 1e-4)
            gain = jnp.exp2(-power) * LEVELS
            for k in range(8):
                level = jnp.round(totals[owner * 8 + k] * gain).astype(jnp.int32).astype(jnp.int16)
                for lh in range(2):
                    first = (k * 2 + lh) * half
                    out_ref[owner, first : first + half, :] = level[:, lh * 128 : (lh + 1) * 128]
            codes = jnp.concatenate(
                [jnp.broadcast_to(power[:, lh * 128 : (lh + 1) * 128], (8, 128)) for lh in range(2)], axis=0
            )
            out_ref[owner, 16 * half :, :] = codes.astype(jnp.int32).astype(jnp.int16)

        return carry

    lax.fori_loop(0, nodes, send_out, 0)


def final_kernel(asked_ref, in_ref, code_ref, table_ref, out_ref, totals, work):
    nodes = in_ref.shape[0]
    orbs, width = out_ref.shape
    half = totals.shape[1] // orbs
    plane = width // half
    pitch = half + 1
    totals[...] = jnp.zeros_like(totals)

    def add_one(node, carry):
        target = asked_ref[node, 0, 0]

        @pl.when(target >= 0)
        def _():
            codes = code_ref[node].astype(jnp.int32).astype(F32)
            start = pl.multiple_of(target * half, half)
            for lh in range(2):
                gain = jnp.exp2(codes[lh * 8 : lh * 8 + 1]) * (1.0 / LEVELS)
                for pos in range(4):
                    first = (pos * 2 + lh) * half
                    level = in_ref[node, first : first + half, :].astype(jnp.int32).astype(F32)
                    totals[pos * 2 + lh, pl.ds(start, half), :] += level * gain

        return carry

    lax.fori_loop(0, nodes, add_one, 0)
    for py in range(2):
        for m in range(2):
            rows = jnp.concatenate([totals[py * 4 + m], totals[py * 4 + 2 + m]], axis=1)
            high, low = halves(rows)
            result = jnp.dot(high, table_ref[py], preferred_element_type=F32) + jnp.dot(
                low, table_ref[py], preferred_element_type=F32
            )
            first = py * 4 + 2 * (1 - m if py else m)
            for j in range(2):
                for orb in range(orbs):
                    work[first + j, orb * pitch : orb * pitch + half, :] = result[
                        orb * half : (orb + 1) * half, j * 128 : (j + 1) * 128
                    ]
    for x in range(half):
        for j in range(plane // 128):
            out_ref[:, x * plane + j * 128 : x * plane + (j + 1) * 128] = work[
                j, pl.ds(x, orbs, stride=pitch), :
            ]


def call_solve(orbs, fetch, offsets, pairs, count, incoming):
    nodes, length, plane = incoming.shape
    half = length // 2
    area = half * half
    tables = host_tables(length)
    smem = pl.BlockSpec(memory_space=pltpu.SMEM)
    hbm = pl.BlockSpec(memory_space=pl.ANY)
    work = pltpu.VMEM((8, length * PITCH, 128), F32)
    return pl.pallas_call(
        functools.partial(solve_kernel, orbs, pairs.shape[0] // 2),
        out_shape=jax.ShapeDtypeStruct((nodes, 16 * half + 16, 128), jnp.int16),
        in_specs=[smem] + [pl.BlockSpec(memory_space=pltpu.VMEM)] * 2 + [hbm],
        out_specs=pl.BlockSpec(memory_space=pltpu.VMEM),
        scratch_shapes=[
            pltpu.VMEM((nodes * 32 + 1, half, area), BF16),
            work,
            pltpu.VMEM((nodes * 8, half, area), F32),
            pltpu.SMEM((BLOCK * 9,), jnp.int32),
            pltpu.SMEM((nodes,), jnp.int32),
            pltpu.VMEM((3 * area, area), BF16),
            pltpu.VMEM((8, half + 8, 128), F32),
            pltpu.VMEM((3, half, area), F32),
            pltpu.SemaphoreType.DMA,
        ],
        compiler_params=pltpu.CompilerParams(vmem_limit_bytes=(10 << 20) + nodes * (704 << 10)),
        name="solve",
    )(
        jnp.concatenate([count, fetch, offsets, pairs]), incoming, tables["variants"], tables["sines"]
    )


def on_device(phi, offsets, fetch, task_pairs, task_count):
    nodes = lax.axis_size("orb")
    orbs, volume = phi.shape
    length = cube_root(volume)
    half, plane = length // 2, length * length
    tables = host_tables(length)
    smem = pl.BlockSpec(memory_space=pltpu.SMEM)
    vmem = pl.BlockSpec(memory_space=pltpu.VMEM)
    params = pltpu.CompilerParams(vmem_limit_bytes=(12 << 20) + nodes * (384 << 10))
    fetch = fetch.reshape(-1)
    asking = pl.pallas_call(
        ask_kernel,
        out_shape=jax.ShapeDtypeStruct((nodes, 1, 128), jnp.int32),
        in_specs=[smem],
        out_specs=vmem,
        name="ask",
    )(fetch)
    packed = pl.pallas_call(
        pack_kernel,
        out_shape=jax.ShapeDtypeStruct((orbs, length, plane), BF16),
        in_specs=[vmem, vmem],
        out_specs=vmem,
        scratch_shapes=[pltpu.VMEM((plane // 128, (orbs + 1) * length, 128), F32)],
        compiler_params=params,
        name="pack",
    )(phi, tables["pack"])
    asked = lax.all_to_all(asking, "orb", split_axis=0, concat_axis=0, tiled=True)
    outgoing = pl.pallas_call(
        pick_kernel,
        out_shape=jax.ShapeDtypeStruct((nodes, length, plane), BF16),
        in_specs=[smem, vmem],
        out_specs=pl.BlockSpec(memory_space=pl.ANY),
        scratch_shapes=[pltpu.SemaphoreType.DMA((nodes,))],
        compiler_params=params,
        name="pick",
    )(asked, packed)
    incoming = lax.all_to_all(outgoing, "orb", split_axis=0, concat_axis=0, tiled=True)
    partial = call_solve(
        orbs, fetch, offsets.reshape(-1), task_pairs.reshape(-1), task_count, incoming
    )
    returned = lax.all_to_all(partial, "orb", split_axis=0, concat_axis=0, tiled=True)
    return pl.pallas_call(
        final_kernel,
        grid=(2,),
        out_shape=jax.ShapeDtypeStruct((orbs, volume), F32),
        in_specs=[
            smem,
            pl.BlockSpec((nodes, 8 * half, 128), lambda hx: (0, hx, 0)),
            pl.BlockSpec((nodes, 16, 128), lambda hx: (0, half, 0)),
            pl.BlockSpec((2, plane // 4, plane // 4), lambda hx: (0, 0, 0)),
        ],
        out_specs=pl.BlockSpec((orbs, volume // 2), lambda hx: (0, hx)),
        scratch_shapes=[
            pltpu.VMEM((8, orbs * half, 128), F32),
            pltpu.VMEM((plane // 128, orbs * (half + 1), 128), F32),
        ],
        compiler_params=params,
        name="final",
    )(asked, returned, returned, tables["unpack"])


def solution(mesh):
    in_specs = (
        P(("groups", "orb"), None),
        P("groups", None),
        P(("groups", "orb"), None),
        P(("groups", "orb"), None),
        P(("groups", "orb")),
    )
    out_specs = P(("groups", "orb"), None)
    return jax.shard_map(
        on_device, mesh=mesh, in_specs=in_specs, out_specs=out_specs, check_vma=False
    )
```

```python
import functools

import jax
import jax.numpy as jnp
import ml_dtypes
import numpy as np
from jax import lax
from jax.experimental import pallas as pl
from jax.experimental.pallas import tpu as pltpu
from jax.sharding import PartitionSpec as P

BLOCK = 8
PITCH = 9
LEVELS = 32704.0
BF16 = jnp.bfloat16
F32 = jnp.float32


def cube_root(volume):
    length = 1
    while length * length * length < volume:
        length = length + 1
    return length


def split_bf16(values):
    high = values.astype(ml_dtypes.bfloat16)
    low = (values - high.astype(np.float64)).astype(ml_dtypes.bfloat16)
    return high, low


def host_tables(length):
    half = length // 2
    area = half * half
    count = np.arange(length) + 1.0
    eigen = 2.0 - 2.0 * np.cos(np.pi * count / (length + 1))
    modes = [eigen[0::2][::-1], eigen[1::2]]
    near = np.arange(half) + 1.0
    sine = np.sqrt(2.0 / (length + 1)) * np.sin(2.0 * np.pi * np.outer(near, near) / (length + 1))
    high, low = split_bf16(np.kron(sine, sine))
    sines = np.concatenate([high, high, low], axis=0)
    factors = []
    for par_y in (0, 1):
        for par_z in (0, 1):
            beta = 2.0 + (modes[par_y][:, None] + modes[par_z][None, :]).reshape(area)
            rows = [1.0 / beta]
            for _ in range(half - 1):
                rows.append(1.0 / (beta - rows[-1]))
            rows.append(1.0 / (1.0 - rows[-1] ** 2))
            rows.extend([rows[-1]] * 7)
            rows = np.stack(rows).astype(np.float32)
            factors.append(rows)
    place = np.arange(area)
    low_y, low_z = place // half, place % half
    variants = []
    for rev_y, rev_z in ((0, 1), (1, 0), (1, 1)):
        src_y = half - 1 - low_y if rev_y else low_y
        src_z = half - 1 - low_z if rev_z else low_z
        one_hot = np.zeros((area, area), ml_dtypes.bfloat16)
        one_hot[src_y * half + src_z, place] = 1
        variants.append(one_hot)
    wide = 2 * area
    spot = np.arange(wide)
    pack = np.zeros((wide, wide), ml_dtypes.bfloat16)
    z_half, rest = spot // area, spot % area
    pack[(rest // half) * length + z_half * half + rest % half, spot] = 1
    spot = np.arange(area)
    z_half, rest = spot // (area // 2), spot % (area // 2)
    unpack = []
    for par_y in (0, 1):
        y_nat = half // 2 - 1 - rest // half if par_y else rest // half
        z_nat = np.where(z_half == 1, length - 1 - rest % half, rest % half)
        one_hot = np.zeros((area, area), ml_dtypes.bfloat16)
        one_hot[spot, y_nat * length + z_nat] = 1
        unpack.append(one_hot)
    left = np.concatenate(factors).astype(np.float64)
    pieces = []
    for _ in range(3):
        pieces.append(left.astype(ml_dtypes.bfloat16))
        left = left - pieces[-1].astype(np.float64)
    variants = np.concatenate(
        [np.concatenate(variants, axis=1), np.concatenate(pieces, axis=1)], axis=0
    )
    return dict(sines=sines, variants=variants, pack=pack, unpack=np.stack(unpack))


def halves(value):
    high = value.astype(BF16)
    low = (value - high.astype(F32)).astype(BF16)
    return high, low


def ask_kernel(fetch_ref, out_ref):
    for node in range(out_ref.shape[0]):
        out_ref[node] = jnp.full(out_ref.shape[1:], fetch_ref[node], jnp.int32)


def pack_kernel(phi_ref, table_ref, out_ref, work):
    orbs = phi_ref.shape[0]
    length = out_ref.shape[1]
    plane = length * length
    wide = plane // 2
    pitch = orbs + 1
    for y_half in range(2):
        rows = jnp.concatenate(
            [phi_ref[:, x * plane + y_half * wide : x * plane + (y_half + 1) * wide] for x in range(length)],
            axis=0,
        )
        moved = jnp.dot(rows, table_ref[...], preferred_element_type=F32)
        for j in range(wide // 128):
            for x in range(length):
                work[y_half * (wide // 128) + j, x * pitch : x * pitch + orbs, :] = moved[
                    x * orbs : (x + 1) * orbs, j * 128 : (j + 1) * 128
                ]
    for orb in range(orbs):
        for j in range(plane // 128):
            piece = work[j, pl.ds(orb, length, stride=pitch), :]
            out_ref[orb, :, j * 128 : (j + 1) * 128] = piece.astype(BF16)


def pick_kernel(asked_ref, packed_ref, out_ref, sems):
    copies = []
    for node in range(out_ref.shape[0]):
        orb = jnp.maximum(asked_ref[node, 0, 0], 0)
        copies.append(pltpu.make_async_copy(packed_ref.at[orb], out_ref.at[node], sems.at[node]))
        copies[-1].start()
    for copy in copies:
        copy.wait()


def solve_kernel(
    orbs, slots, ints_ref, in_ref, var_ref, sine_hbm,
    out_ref, octs, even_work, odd_work, totals, plan, used, sine_ref, fac_ref, signs, sem,
):
    nodes, length = in_ref.shape[0], in_ref.shape[1]
    half = length // 2
    area = half * half
    zero_at = nodes * 32
    group = 8
    table = pltpu.make_async_copy(sine_hbm, sine_ref, sem)
    table.start()
    row_at = lax.broadcasted_iota(jnp.int32, (half, area), 1)
    turn_z = 1.0 - 2.0 * (row_at % 2).astype(F32)
    turn_y = 1.0 - 2.0 * (row_at // half % 2).astype(F32)
    signs[0] = turn_y * turn_z
    signs[1] = turn_y
    signs[2] = turn_z
    octs[zero_at] = jnp.zeros((half, area), BF16)
    fetch_at, offset_at, pair_at = 1, 1 + nodes, 1 + nodes + nodes * orbs * 3
    live_count = ints_ref[0]
    last_slot = slots - 1

    def make_variants(step, carry):
        for quad in range(4):
            block = in_ref[pl.ds(step * group, group), :, quad * area : (quad + 1) * area]
            turned = jnp.dot(
                block.reshape(group * length, area), var_ref[:area, :], preferred_element_type=F32
            ).astype(BF16)
            for one in range(group):
                for hx in range(2):
                    base = (((step * group + one) * 2 + hx) * 4 + quad) * 4
                    octs[base] = block[one, hx * half : (hx + 1) * half]
                    first = one * length + hx * half
                    for rev in range(3):
                        octs[base + 1 + rev] = turned[first : first + half, rev * area : (rev + 1) * area]
        return carry

    lax.fori_loop(0, nodes // group, make_variants, 0)

    def clear(step, carry):
        for k in range(8):
            totals[step * 8 + k] = jnp.zeros((half, area), F32)
        used[step] = 0
        return carry

    lax.fori_loop(0, nodes, clear, 0)

    def multiply(work, slot, t):
        at = jnp.minimum(slot, last_slot)
        first, second = ints_ref[pair_at + 2 * at], ints_ref[pair_at + 2 * at + 1]
        id_a = first * orbs + jnp.maximum(ints_ref[fetch_at + first], 0)
        id_b = second * orbs + jnp.maximum(ints_ref[fetch_at + second], 0)
        shift = [ints_ref[offset_at + id_a * 3 + k] - ints_ref[offset_at + id_b * 3 + k] for k in range(3)]
        fits = [[(side + shift[k] >= 0) & (side + shift[k] < 2) for side in range(2)] for k in range(3)]
        start = second * 32 + shift[0] * 16 + shift[1] * 8 + shift[2] * 4
        live = slot < live_count
        note = (slot + BLOCK) * 9
        plan[note] = first
        used[first] = jnp.where(live, 1, used[first])
        for hx in range(2):
            dens = []
            for pos in range(4):
                py, pz = pos // 2, pos % 2
                inside = live & fits[0][hx] & fits[1][py] & fits[2][pz]
                spot = jnp.where(inside, start + (hx * 16 + py * 8 + pz * 4 + pos), zero_at)
                plan[note + 1 + hx * 4 + pos] = spot
                own = octs[first * 32 + (hx * 16 + pos * 5)].astype(F32)
                dens.append(own * octs[spot].astype(F32))
            even0, odd0 = dens[0] + dens[1], dens[0] - dens[1]
            even1, odd1 = dens[2] + dens[3], dens[2] - dens[3]
            folded = (
                (even0 + even1) * signs[0],
                (odd0 + odd1) * signs[1],
                (even0 - even1) * signs[2],
                odd0 - odd1,
            )
            for cls in range(4):
                for lh in range(2):
                    work[cls * 2 + lh, pl.ds(hx * half * PITCH + t, half, stride=PITCH), :] = folded[cls][
                        :, lh * 128 : (lh + 1) * 128
                    ]

    def gather(work, slot, t):
        note = (slot + BLOCK) * 9
        first = plan[note] * 8
        for hx in range(2):
            folded = []
            for cls in range(4):
                pieces = [
                    work[cls * 2 + lh, pl.ds(hx * half * PITCH + t, half, stride=PITCH), :] for lh in range(2)
                ]
                piece = jnp.concatenate(pieces, axis=1)
                folded.append(piece * signs[cls] if cls < 3 else piece)
            sum0, dif0 = folded[0] + folded[1], folded[0] - folded[1]
            sum1, dif1 = folded[2] + folded[3], folded[2] - folded[3]
            potential = (sum0 + sum1, dif0 + dif1, sum0 - sum1, dif0 - dif1)
            for pos in range(4):
                moved = octs[plan[note + 1 + hx * 4 + pos]].astype(F32)
                totals[first + (hx * 4 + pos)] += potential[pos] * moved

    def begin(work, cls):
        both = jnp.concatenate(
            [
                jnp.concatenate(
                    [work[cls * 2 + lh, x * PITCH : x * PITCH + BLOCK, :] for x in range(length)], axis=0
                )
                for lh in range(2)
            ],
            axis=1,
        )
        high, low = halves(both)
        return jnp.dot(
            jnp.concatenate([high, low, high], axis=1), sine_ref[...], preferred_element_type=F32
        )

    def finish(work, cls, result):
        for x in range(length):
            for lh in range(2):
                work[cls * 2 + lh, x * PITCH : x * PITCH + BLOCK, :] = result[
                    x * BLOCK : (x + 1) * BLOCK, lh * 128 : (lh + 1) * 128
                ]

    def sweep(work, chains):
        def rows(x):
            return slice(x * PITCH, x * PITCH + BLOCK)

        def factor(ch, x):
            return jnp.broadcast_to(fac_ref[ch, x : x + 1, :], (BLOCK, 128))

        low, high = {}, {}
        for x in range(half):
            far = length - 1 - x
            for ch in chains:
                scale = factor(ch, x)
                from_low, from_high = work[ch, rows(x), :], work[ch, rows(far), :]
                if x > 0:
                    from_low, from_high = from_low + low[ch], from_high + high[ch]
                low[ch], high[ch] = from_low * scale, from_high * scale
                if x < half - 1:
                    work[ch, rows(x), :] = low[ch]
                    work[ch, rows(far), :] = high[ch]
        for ch in chains:
            scale, meet = factor(ch, half - 1), factor(ch, half)
            low[ch], high[ch] = (low[ch] + scale * high[ch]) * meet, (high[ch] + scale * low[ch]) * meet
            work[ch, rows(half - 1), :] = low[ch]
            work[ch, rows(half), :] = high[ch]
        for x in range(half - 2, -1, -1):
            far = length - 1 - x
            for ch in chains:
                scale = factor(ch, x)
                low[ch] = work[ch, rows(x), :] + scale * low[ch]
                high[ch] = work[ch, rows(far), :] + scale * high[ch]
                work[ch, rows(x), :] = low[ch]
                work[ch, rows(far), :] = high[ch]

    def half_step(work, other, before, after):
        share = BLOCK // 4
        for cls in range(4):
            result = begin(work, cls)
            if before is not None:
                for t in range(cls * share, (cls + 1) * share):
                    gather(other, before * BLOCK + t, t)
            if cls == 2:
                sweep(work, range(4))
            finish(work, cls, result)
        for cls in range(4):
            result = begin(work, cls)
            if cls == 0:
                sweep(work, range(4, 8))
            if after is not None:
                for t in range(cls * share, (cls + 1) * share):
                    multiply(other, after * BLOCK + t, t)
            finish(work, cls, result)

    for t in range(BLOCK):
        multiply(even_work, t, t)
    table.wait()
    steps = fac_ref.shape[1]
    terms = [var_ref[area:, k * area : (k + 1) * area].astype(F32) for k in range(3)]
    joined = (terms[2] + terms[1]) + terms[0]
    for ch in range(8):
        first, lanes = ch // 2 * steps, ch % 2 * 128
        fac_ref[ch] = joined[first : first + steps, lanes : lanes + 128]

    def run_pair(step, carry):
        half_step(odd_work, even_work, 2 * step, 2 * step + 2)
        half_step(even_work, odd_work, 2 * step + 1, 2 * step + 3)
        return carry

    pairs = (live_count + 2 * BLOCK - 1) // (2 * BLOCK)
    half_step(even_work, odd_work, None, 1)
    lax.fori_loop(0, pairs - 1, run_pair, 0)
    half_step(odd_work, even_work, 2 * pairs - 2, None)
    for t in range(BLOCK):
        gather(odd_work, (2 * pairs - 1) * BLOCK + t, t)

    def send_out(owner, carry):
        @pl.when(used[owner] == 0)
        def _():
            out_ref[owner] = jnp.zeros(out_ref.shape[1:], jnp.int16)

        @pl.when(used[owner] > 0)
        def _():
            top = jnp.abs(totals[owner * 8])
            for k in range(1, 8):
                top = jnp.maximum(top, jnp.abs(totals[owner * 8 + k]))
            top = jnp.maximum(jnp.max(top, axis=0, keepdims=True), 2.0**-110)
            power = jnp.ceil(jnp.log2(top) + 1e-4)
            gain = jnp.exp2(-power) * LEVELS
            for k in range(8):
                level = jnp.round(totals[owner * 8 + k] * gain).astype(jnp.int32).astype(jnp.int16)
                for lh in range(2):
                    first = (k * 2 + lh) * half
                    out_ref[owner, first : first + half, :] = level[:, lh * 128 : (lh + 1) * 128]
            codes = jnp.concatenate(
                [jnp.broadcast_to(power[:, lh * 128 : (lh + 1) * 128], (8, 128)) for lh in range(2)], axis=0
            )
            out_ref[owner, 16 * half :, :] = codes.astype(jnp.int32).astype(jnp.int16)

        return carry

    lax.fori_loop(0, nodes, send_out, 0)


def final_kernel(asked_ref, in_ref, code_ref, table_ref, out_ref, totals, work):
    nodes = in_ref.shape[0]
    orbs, width = out_ref.shape
    half = totals.shape[1] // orbs
    plane = width // half
    pitch = half + 1
    totals[...] = jnp.zeros_like(totals)

    def add_one(node, carry):
        target = asked_ref[node, 0, 0]

        @pl.when(target >= 0)
        def _():
            codes = code_ref[node].astype(jnp.int32).astype(F32)
            start = pl.multiple_of(target * half, half)
            for lh in range(2):
                gain = jnp.exp2(codes[lh * 8 : lh * 8 + 1]) * (1.0 / LEVELS)
                for pos in range(4):
                    first = (pos * 2 + lh) * half
                    level = in_ref[node, first : first + half, :].astype(jnp.int32).astype(F32)
                    totals[pos * 2 + lh, pl.ds(start, half), :] += level * gain

        return carry

    lax.fori_loop(0, nodes, add_one, 0)
    for py in range(2):
        for m in range(2):
            rows = jnp.concatenate([totals[py * 4 + m], totals[py * 4 + 2 + m]], axis=1)
            high, low = halves(rows)
            result = jnp.dot(high, table_ref[py], preferred_element_type=F32) + jnp.dot(
                low, table_ref[py], preferred_element_type=F32
            )
            first = py * 4 + 2 * (1 - m if py else m)
            for j in range(2):
                for orb in range(orbs):
                    work[first + j, orb * pitch : orb * pitch + half, :] = result[
                        orb * half : (orb + 1) * half, j * 128 : (j + 1) * 128
                    ]
    for x in range(half):
        for j in range(plane // 128):
            out_ref[:, x * plane + j * 128 : x * plane + (j + 1) * 128] = work[
                j, pl.ds(x, orbs, stride=pitch), :
            ]


def call_solve(orbs, fetch, offsets, pairs, count, incoming):
    nodes, length, plane = incoming.shape
    half = length // 2
    area = half * half
    tables = host_tables(length)
    smem = pl.BlockSpec(memory_space=pltpu.SMEM)
    hbm = pl.BlockSpec(memory_space=pl.ANY)
    work = pltpu.VMEM((8, length * PITCH, 128), F32)
    steps = (pairs.shape[0] // 2 + 2 * BLOCK - 1) // (2 * BLOCK)
    return pl.pallas_call(
        functools.partial(solve_kernel, orbs, pairs.shape[0] // 2),
        out_shape=jax.ShapeDtypeStruct((nodes, 16 * half + 16, 128), jnp.int16),
        in_specs=[smem] + [pl.BlockSpec(memory_space=pltpu.VMEM)] * 2 + [hbm],
        out_specs=pl.BlockSpec(memory_space=pltpu.VMEM),
        scratch_shapes=[
            pltpu.VMEM((nodes * 32 + 1, half, area), BF16),
            work,
            work,
            pltpu.VMEM((nodes * 8, half, area), F32),
            pltpu.SMEM(((2 * steps + 2) * BLOCK * 9,), jnp.int32),
            pltpu.SMEM((nodes,), jnp.int32),
            pltpu.VMEM((3 * area, area), BF16),
            pltpu.VMEM((8, half + 8, 128), F32),
            pltpu.VMEM((3, half, area), F32),
            pltpu.SemaphoreType.DMA,
        ],
        compiler_params=pltpu.CompilerParams(vmem_limit_bytes=(10 << 20) + nodes * (704 << 10)),
        name="solve",
    )(
        jnp.concatenate([count, fetch, offsets, pairs]), incoming, tables["variants"], tables["sines"]
    )


def on_device(phi, offsets, fetch, task_pairs, task_count):
    nodes = lax.axis_size("orb")
    orbs, volume = phi.shape
    length = cube_root(volume)
    half, plane = length // 2, length * length
    tables = host_tables(length)
    smem = pl.BlockSpec(memory_space=pltpu.SMEM)
    vmem = pl.BlockSpec(memory_space=pltpu.VMEM)
    params = pltpu.CompilerParams(vmem_limit_bytes=(12 << 20) + nodes * (384 << 10))
    fetch = fetch.reshape(-1)
    asking = pl.pallas_call(
        ask_kernel,
        out_shape=jax.ShapeDtypeStruct((nodes, 1, 128), jnp.int32),
        in_specs=[smem],
        out_specs=vmem,
        name="ask",
    )(fetch)
    packed = pl.pallas_call(
        pack_kernel,
        out_shape=jax.ShapeDtypeStruct((orbs, length, plane), BF16),
        in_specs=[vmem, vmem],
        out_specs=vmem,
        scratch_shapes=[pltpu.VMEM((plane // 128, (orbs + 1) * length, 128), F32)],
        compiler_params=params,
        name="pack",
    )(phi, tables["pack"])
    asked = lax.all_to_all(asking, "orb", split_axis=0, concat_axis=0, tiled=True)
    outgoing = pl.pallas_call(
        pick_kernel,
        out_shape=jax.ShapeDtypeStruct((nodes, length, plane), BF16),
        in_specs=[smem, vmem],
        out_specs=pl.BlockSpec(memory_space=pl.ANY),
        scratch_shapes=[pltpu.SemaphoreType.DMA((nodes,))],
        compiler_params=params,
        name="pick",
    )(asked, packed)
    incoming = lax.all_to_all(outgoing, "orb", split_axis=0, concat_axis=0, tiled=True)
    partial = call_solve(
        orbs, fetch, offsets.reshape(-1), task_pairs.reshape(-1), task_count, incoming
    )
    returned = lax.all_to_all(partial, "orb", split_axis=0, concat_axis=0, tiled=True)
    return pl.pallas_call(
        final_kernel,
        grid=(2,),
        out_shape=jax.ShapeDtypeStruct((orbs, volume), F32),
        in_specs=[
            smem,
            pl.BlockSpec((nodes, 8 * half, 128), lambda hx: (0, hx, 0)),
            pl.BlockSpec((nodes, 16, 128), lambda hx: (0, half, 0)),
            pl.BlockSpec((2, plane // 4, plane // 4), lambda hx: (0, 0, 0)),
        ],
        out_specs=pl.BlockSpec((orbs, volume // 2), lambda hx: (0, hx)),
        scratch_shapes=[
            pltpu.VMEM((8, orbs * half, 128), F32),
            pltpu.VMEM((plane // 128, orbs * (half + 1), 128), F32),
        ],
        compiler_params=params,
        name="final",
    )(asked, returned, returned, tables["unpack"])


def solution(mesh):
    in_specs = (
        P(("groups", "orb"), None),
        P("groups", None),
        P(("groups", "orb"), None),
        P(("groups", "orb"), None),
        P(("groups", "orb")),
    )
    out_specs = P(("groups", "orb"), None)
    return jax.shard_map(
        on_device, mesh=mesh, in_specs=in_specs, out_specs=out_specs, check_vma=False
    )
```

```python
import functools

import jax
import jax.numpy as jnp
import ml_dtypes
import numpy as np
from jax import lax
from jax.experimental import pallas as pl
from jax.experimental.pallas import tpu as pltpu
from jax.sharding import PartitionSpec as P

BLOCK = 8
PITCH = 9
LEVELS = 32704.0
BF16 = jnp.bfloat16
F32 = jnp.float32


def cube_root(volume):
    length = 1
    while length * length * length < volume:
        length = length + 1
    return length


def split_bf16(values):
    high = values.astype(ml_dtypes.bfloat16)
    low = (values - high.astype(np.float64)).astype(ml_dtypes.bfloat16)
    return high, low


def host_tables(length):
    half = length // 2
    area = half * half
    count = np.arange(length) + 1.0
    eigen = 2.0 - 2.0 * np.cos(np.pi * count / (length + 1))
    modes = [eigen[0::2][::-1], eigen[1::2]]
    near = np.arange(half) + 1.0
    sine = np.sqrt(2.0 / (length + 1)) * np.sin(2.0 * np.pi * np.outer(near, near) / (length + 1))
    high, low = split_bf16(np.kron(sine, sine))
    sines = np.concatenate([high, high, low], axis=0)
    factors = []
    for par_y in (0, 1):
        for par_z in (0, 1):
            beta = 2.0 + (modes[par_y][:, None] + modes[par_z][None, :]).reshape(area)
            rows = [1.0 / beta]
            for _ in range(half - 1):
                rows.append(1.0 / (beta - rows[-1]))
            rows.append(1.0 / (1.0 - rows[-1] ** 2))
            rows.extend([rows[-1]] * 7)
            rows = np.stack(rows).astype(np.float32)
            factors.append(rows)
    place = np.arange(area)
    low_y, low_z = place // half, place % half
    variants = []
    for rev_y, rev_z in ((0, 1), (1, 0), (1, 1)):
        src_y = half - 1 - low_y if rev_y else low_y
        src_z = half - 1 - low_z if rev_z else low_z
        one_hot = np.zeros((area, area), ml_dtypes.bfloat16)
        one_hot[src_y * half + src_z, place] = 1
        variants.append(one_hot)
    spot = np.arange(area)
    z_half, rest = spot // (area // 2), spot % (area // 2)
    pack = np.zeros((area, area), ml_dtypes.bfloat16)
    pack[(rest // half) * length + z_half * half + rest % half, spot] = 1
    spot = np.arange(area)
    z_half, rest = spot // (area // 2), spot % (area // 2)
    unpack = []
    for par_y in (0, 1):
        y_nat = half // 2 - 1 - rest // half if par_y else rest // half
        z_nat = np.where(z_half == 1, length - 1 - rest % half, rest % half)
        one_hot = np.zeros((area, area), ml_dtypes.bfloat16)
        one_hot[spot, y_nat * length + z_nat] = 1
        unpack.append(one_hot)
    left = np.concatenate(factors).astype(np.float64)
    pieces = []
    for _ in range(3):
        pieces.append(left.astype(ml_dtypes.bfloat16))
        left = left - pieces[-1].astype(np.float64)
    variants = np.concatenate(
        [np.concatenate(variants, axis=1), np.concatenate(pieces, axis=1)], axis=0
    )
    return dict(sines=sines, variants=variants, pack=pack, unpack=np.stack(unpack))


def halves(value):
    high = value.astype(BF16)
    low = (value - high.astype(F32)).astype(BF16)
    return high, low


def ask_kernel(fetch_ref, out_ref):
    for node in range(out_ref.shape[0]):
        out_ref[node] = jnp.full(out_ref.shape[1:], fetch_ref[node], jnp.int32)


def pack_kernel(phi_ref, table_ref, out_ref, work):
    orbs = phi_ref.shape[0]
    length = out_ref.shape[1]
    plane = length * length
    pitch = orbs + 1
    area = plane // 4
    for quarter in range(4):
        rows = jnp.concatenate(
            [phi_ref[:, x * plane + quarter * area : x * plane + (quarter + 1) * area] for x in range(length)],
            axis=0,
        )
        moved = jnp.dot(rows, table_ref[...], preferred_element_type=F32)
        for side in range(2):
            j = quarter // 2 * 4 + side * 2 + quarter % 2
            for x in range(length):
                work[j, x * pitch : x * pitch + orbs, :] = moved[
                    x * orbs : (x + 1) * orbs, side * 128 : (side + 1) * 128
                ]
    for orb in range(orbs):
        for j in range(plane // 128):
            piece = work[j, pl.ds(orb, length, stride=pitch), :]
            out_ref[orb, :, j * 128 : (j + 1) * 128] = piece.astype(BF16)


def pick_kernel(asked_ref, packed_ref, out_ref, sems):
    copies = []
    for node in range(out_ref.shape[0]):
        orb = jnp.maximum(asked_ref[node, 0, 0], 0)
        copies.append(pltpu.make_async_copy(packed_ref.at[orb], out_ref.at[node], sems.at[node]))
        copies[-1].start()
    for copy in copies:
        copy.wait()


def solve_kernel(
    orbs, slots, ints_ref, in_ref, var_ref, sine_hbm,
    out_ref, octs, even_work, odd_work, totals, plan, used, sine_ref, fac_ref, signs, sem,
):
    nodes, length = in_ref.shape[0], in_ref.shape[1]
    half = length // 2
    area = half * half
    zero_at = nodes * 32
    group = 8
    table = pltpu.make_async_copy(sine_hbm, sine_ref, sem)
    table.start()
    row_at = lax.broadcasted_iota(jnp.int32, (half, area), 1)
    turn_z = 1.0 - 2.0 * (row_at % 2).astype(F32)
    turn_y = 1.0 - 2.0 * (row_at // half % 2).astype(F32)
    signs[0] = turn_y * turn_z
    signs[1] = turn_y
    signs[2] = turn_z
    octs[zero_at] = jnp.zeros((half, area), BF16)
    fetch_at, offset_at, pair_at = 1, 1 + nodes, 1 + nodes + nodes * orbs * 3
    live_count = ints_ref[0]
    last_slot = slots - 1

    def make_variants(step, carry):
        for quad in range(4):
            block = in_ref[pl.ds(step * group, group), :, quad * area : (quad + 1) * area]
            turned = jnp.dot(
                block.reshape(group * length, area), var_ref[:area, :], preferred_element_type=F32
            ).astype(BF16)
            for one in range(group):
                for hx in range(2):
                    base = (((step * group + one) * 2 + hx) * 4 + quad) * 4
                    octs[base] = block[one, hx * half : (hx + 1) * half]
                    first = one * length + hx * half
                    for rev in range(3):
                        octs[base + 1 + rev] = turned[first : first + half, rev * area : (rev + 1) * area]
        return carry

    lax.fori_loop(0, nodes // group, make_variants, 0)

    def clear(step, carry):
        for k in range(8):
            totals[step * 8 + k] = jnp.zeros((half, area), F32)
        used[step] = 0
        return carry

    lax.fori_loop(0, nodes, clear, 0)

    def multiply(work, slot, t):
        at = jnp.minimum(slot, last_slot)
        first, second = ints_ref[pair_at + 2 * at], ints_ref[pair_at + 2 * at + 1]
        id_a = first * orbs + jnp.maximum(ints_ref[fetch_at + first], 0)
        id_b = second * orbs + jnp.maximum(ints_ref[fetch_at + second], 0)
        shift = [ints_ref[offset_at + id_a * 3 + k] - ints_ref[offset_at + id_b * 3 + k] for k in range(3)]
        fits = [[(side + shift[k] >= 0) & (side + shift[k] < 2) for side in range(2)] for k in range(3)]
        start = second * 32 + shift[0] * 16 + shift[1] * 8 + shift[2] * 4
        live = slot < live_count
        note = (slot + BLOCK) * 9
        plan[note] = first
        used[first] = jnp.where(live, 1, used[first])
        for hx in range(2):
            dens = []
            for pos in range(4):
                py, pz = pos // 2, pos % 2
                inside = live & fits[0][hx] & fits[1][py] & fits[2][pz]
                spot = jnp.where(inside, start + (hx * 16 + py * 8 + pz * 4 + pos), zero_at)
                plan[note + 1 + hx * 4 + pos] = spot
                own = octs[first * 32 + (hx * 16 + pos * 5)].astype(F32)
                dens.append(own * octs[spot].astype(F32))
            even0, odd0 = dens[0] + dens[1], dens[0] - dens[1]
            even1, odd1 = dens[2] + dens[3], dens[2] - dens[3]
            folded = (
                (even0 + even1) * signs[0],
                (odd0 + odd1) * signs[1],
                (even0 - even1) * signs[2],
                odd0 - odd1,
            )
            for cls in range(4):
                for lh in range(2):
                    work[cls * 2 + lh, pl.ds(hx * half * PITCH + t, half, stride=PITCH), :] = folded[cls][
                        :, lh * 128 : (lh + 1) * 128
                    ]

    def gather(work, slot, t):
        note = (slot + BLOCK) * 9
        first = plan[note] * 8
        for hx in range(2):
            folded = []
            for cls in range(4):
                pieces = [
                    work[cls * 2 + lh, pl.ds(hx * half * PITCH + t, half, stride=PITCH), :] for lh in range(2)
                ]
                piece = jnp.concatenate(pieces, axis=1)
                folded.append(piece * signs[cls] if cls < 3 else piece)
            sum0, dif0 = folded[0] + folded[1], folded[0] - folded[1]
            sum1, dif1 = folded[2] + folded[3], folded[2] - folded[3]
            potential = (sum0 + sum1, dif0 + dif1, sum0 - sum1, dif0 - dif1)
            for pos in range(4):
                moved = octs[plan[note + 1 + hx * 4 + pos]].astype(F32)
                totals[first + (hx * 4 + pos)] += potential[pos] * moved

    def begin(work, cls):
        both = jnp.concatenate(
            [
                jnp.concatenate(
                    [work[cls * 2 + lh, x * PITCH : x * PITCH + BLOCK, :] for x in range(length)], axis=0
                )
                for lh in range(2)
            ],
            axis=1,
        )
        high, low = halves(both)
        return jnp.dot(
            jnp.concatenate([high, low, high], axis=1), sine_ref[...], preferred_element_type=F32
        )

    def finish(work, cls, result):
        for x in range(length):
            for lh in range(2):
                work[cls * 2 + lh, x * PITCH : x * PITCH + BLOCK, :] = result[
                    x * BLOCK : (x + 1) * BLOCK, lh * 128 : (lh + 1) * 128
                ]

    def sweep(work, chains):
        def rows(x):
            return slice(x * PITCH, x * PITCH + BLOCK)

        def factor(ch, x):
            return jnp.broadcast_to(fac_ref[ch, x : x + 1, :], (BLOCK, 128))

        low, high = {}, {}
        for x in range(half):
            far = length - 1 - x
            for ch in chains:
                scale = factor(ch, x)
                from_low, from_high = work[ch, rows(x), :], work[ch, rows(far), :]
                if x > 0:
                    from_low, from_high = from_low + low[ch], from_high + high[ch]
                low[ch], high[ch] = from_low * scale, from_high * scale
                if x < half - 1:
                    work[ch, rows(x), :] = low[ch]
                    work[ch, rows(far), :] = high[ch]
        for ch in chains:
            scale, meet = factor(ch, half - 1), factor(ch, half)
            low[ch], high[ch] = (low[ch] + scale * high[ch]) * meet, (high[ch] + scale * low[ch]) * meet
            work[ch, rows(half - 1), :] = low[ch]
            work[ch, rows(half), :] = high[ch]
        for x in range(half - 2, -1, -1):
            far = length - 1 - x
            for ch in chains:
                scale = factor(ch, x)
                low[ch] = work[ch, rows(x), :] + scale * low[ch]
                high[ch] = work[ch, rows(far), :] + scale * high[ch]
                work[ch, rows(x), :] = low[ch]
                work[ch, rows(far), :] = high[ch]

    def half_step(work, other, before, after):
        share = BLOCK // 4
        for cls in range(4):
            result = begin(work, cls)
            if before is not None:
                for t in range(cls * share, (cls + 1) * share):
                    gather(other, before * BLOCK + t, t)
            if cls == 2:
                sweep(work, range(4))
            finish(work, cls, result)
        for cls in range(4):
            result = begin(work, cls)
            if cls == 0:
                sweep(work, range(4, 8))
            if after is not None:
                for t in range(cls * share, (cls + 1) * share):
                    multiply(other, after * BLOCK + t, t)
            finish(work, cls, result)

    for t in range(BLOCK):
        multiply(even_work, t, t)
    table.wait()
    steps = fac_ref.shape[1]
    terms = [var_ref[area:, k * area : (k + 1) * area].astype(F32) for k in range(3)]
    joined = (terms[2] + terms[1]) + terms[0]
    for ch in range(8):
        first, lanes = ch // 2 * steps, ch % 2 * 128
        fac_ref[ch] = joined[first : first + steps, lanes : lanes + 128]

    def run_pair(step, carry):
        half_step(odd_work, even_work, 2 * step, 2 * step + 2)
        half_step(even_work, odd_work, 2 * step + 1, 2 * step + 3)
        return carry

    pairs = (live_count + 2 * BLOCK - 1) // (2 * BLOCK)
    half_step(even_work, odd_work, None, 1)
    lax.fori_loop(0, pairs - 1, run_pair, 0)
    half_step(odd_work, even_work, 2 * pairs - 2, None)
    for t in range(BLOCK):
        gather(odd_work, (2 * pairs - 1) * BLOCK + t, t)

    def send_out(owner, carry):
        @pl.when(used[owner] == 0)
        def _():
            out_ref[owner] = jnp.zeros(out_ref.shape[1:], jnp.int16)

        @pl.when(used[owner] > 0)
        def _():
            top = jnp.abs(totals[owner * 8])
            for k in range(1, 8):
                top = jnp.maximum(top, jnp.abs(totals[owner * 8 + k]))
            top = jnp.maximum(jnp.max(top, axis=0, keepdims=True), 2.0**-110)
            power = jnp.ceil(jnp.log2(top) + 1e-4)
            gain = jnp.exp2(-power) * LEVELS
            for k in range(8):
                level = jnp.round(totals[owner * 8 + k] * gain).astype(jnp.int32).astype(jnp.int16)
                for lh in range(2):
                    first = (k * 2 + lh) * half
                    out_ref[owner, first : first + half, :] = level[:, lh * 128 : (lh + 1) * 128]
            codes = jnp.concatenate(
                [jnp.broadcast_to(power[:, lh * 128 : (lh + 1) * 128], (8, 128)) for lh in range(2)], axis=0
            )
            out_ref[owner, 16 * half :, :] = codes.astype(jnp.int32).astype(jnp.int16)

        return carry

    lax.fori_loop(0, nodes, send_out, 0)


def final_kernel(asked_ref, in_ref, code_ref, table_ref, out_ref, totals, work):
    nodes = in_ref.shape[0]
    orbs, width = out_ref.shape
    half = totals.shape[1] // orbs
    plane = width // half
    pitch = half + 1
    totals[...] = jnp.zeros_like(totals)

    def add_one(node, carry):
        target = asked_ref[node, 0, 0]

        @pl.when(target >= 0)
        def _():
            codes = code_ref[node].astype(jnp.int32).astype(F32)
            start = pl.multiple_of(target * half, half)
            for lh in range(2):
                gain = jnp.exp2(codes[lh * 8 : lh * 8 + 1]) * (1.0 / LEVELS)
                for pos in range(4):
                    first = (pos * 2 + lh) * half
                    level = in_ref[node, first : first + half, :].astype(jnp.int32).astype(F32)
                    totals[pos * 2 + lh, pl.ds(start, half), :] += level * gain

        return carry

    lax.fori_loop(0, nodes, add_one, 0)
    for py in range(2):
        for m in range(2):
            rows = jnp.concatenate([totals[py * 4 + m], totals[py * 4 + 2 + m]], axis=1)
            high, low = halves(rows)
            result = jnp.dot(high, table_ref[py], preferred_element_type=F32) + jnp.dot(
                low, table_ref[py], preferred_element_type=F32
            )
            first = py * 4 + 2 * (1 - m if py else m)
            for j in range(2):
                for orb in range(orbs):
                    work[first + j, orb * pitch : orb * pitch + half, :] = result[
                        orb * half : (orb + 1) * half, j * 128 : (j + 1) * 128
                    ]
    for x in range(half):
        for j in range(plane // 128):
            out_ref[:, x * plane + j * 128 : x * plane + (j + 1) * 128] = work[
                j, pl.ds(x, orbs, stride=pitch), :
            ]


def call_solve(orbs, fetch, offsets, pairs, count, incoming):
    nodes, length, plane = incoming.shape
    half = length // 2
    area = half * half
    tables = host_tables(length)
    smem = pl.BlockSpec(memory_space=pltpu.SMEM)
    hbm = pl.BlockSpec(memory_space=pl.ANY)
    work = pltpu.VMEM((8, length * PITCH, 128), F32)
    steps = (pairs.shape[0] // 2 + 2 * BLOCK - 1) // (2 * BLOCK)
    return pl.pallas_call(
        functools.partial(solve_kernel, orbs, pairs.shape[0] // 2),
        out_shape=jax.ShapeDtypeStruct((nodes, 16 * half + 16, 128), jnp.int16),
        in_specs=[smem] + [pl.BlockSpec(memory_space=pltpu.VMEM)] * 2 + [hbm],
        out_specs=pl.BlockSpec(memory_space=pltpu.VMEM),
        scratch_shapes=[
            pltpu.VMEM((nodes * 32 + 1, half, area), BF16),
            work,
            work,
            pltpu.VMEM((nodes * 8, half, area), F32),
            pltpu.SMEM(((2 * steps + 2) * BLOCK * 9,), jnp.int32),
            pltpu.SMEM((nodes,), jnp.int32),
            pltpu.VMEM((3 * area, area), BF16),
            pltpu.VMEM((8, half + 8, 128), F32),
            pltpu.VMEM((3, half, area), F32),
            pltpu.SemaphoreType.DMA,
        ],
        compiler_params=pltpu.CompilerParams(vmem_limit_bytes=(10 << 20) + nodes * (704 << 10)),
        name="solve",
    )(
        jnp.concatenate([count, fetch, offsets, pairs]), incoming, tables["variants"], tables["sines"]
    )


def on_device(phi, offsets, fetch, task_pairs, task_count):
    nodes = lax.axis_size("orb")
    orbs, volume = phi.shape
    length = cube_root(volume)
    half, plane = length // 2, length * length
    tables = host_tables(length)
    smem = pl.BlockSpec(memory_space=pltpu.SMEM)
    vmem = pl.BlockSpec(memory_space=pltpu.VMEM)
    params = pltpu.CompilerParams(vmem_limit_bytes=(12 << 20) + nodes * (384 << 10))
    fetch = fetch.reshape(-1)
    asking = pl.pallas_call(
        ask_kernel,
        out_shape=jax.ShapeDtypeStruct((nodes, 1, 128), jnp.int32),
        in_specs=[smem],
        out_specs=vmem,
        name="ask",
    )(fetch)
    packed = pl.pallas_call(
        pack_kernel,
        out_shape=jax.ShapeDtypeStruct((orbs, length, plane), BF16),
        in_specs=[vmem, vmem],
        out_specs=vmem,
        scratch_shapes=[pltpu.VMEM((plane // 128, (orbs + 1) * length, 128), F32)],
        compiler_params=params,
        name="pack",
    )(phi, tables["pack"])
    asked = lax.all_to_all(asking, "orb", split_axis=0, concat_axis=0, tiled=True)
    outgoing = pl.pallas_call(
        pick_kernel,
        out_shape=jax.ShapeDtypeStruct((nodes, length, plane), BF16),
        in_specs=[smem, vmem],
        out_specs=pl.BlockSpec(memory_space=pl.ANY),
        scratch_shapes=[pltpu.SemaphoreType.DMA((nodes,))],
        compiler_params=params,
        name="pick",
    )(asked, packed)
    incoming = lax.all_to_all(outgoing, "orb", split_axis=0, concat_axis=0, tiled=True)
    partial = call_solve(
        orbs, fetch, offsets.reshape(-1), task_pairs.reshape(-1), task_count, incoming
    )
    returned = lax.all_to_all(partial, "orb", split_axis=0, concat_axis=0, tiled=True)
    return pl.pallas_call(
        final_kernel,
        grid=(2,),
        out_shape=jax.ShapeDtypeStruct((orbs, volume), F32),
        in_specs=[
            smem,
            pl.BlockSpec((nodes, 8 * half, 128), lambda hx: (0, hx, 0)),
            pl.BlockSpec((nodes, 16, 128), lambda hx: (0, half, 0)),
            pl.BlockSpec((2, plane // 4, plane // 4), lambda hx: (0, 0, 0)),
        ],
        out_specs=pl.BlockSpec((orbs, volume // 2), lambda hx: (0, hx)),
        scratch_shapes=[
            pltpu.VMEM((8, orbs * half, 128), F32),
            pltpu.VMEM((plane // 128, orbs * (half + 1), 128), F32),
        ],
        compiler_params=params,
        name="final",
    )(asked, returned, returned, tables["unpack"])


def solution(mesh):
    in_specs = (
        P(("groups", "orb"), None),
        P("groups", None),
        P(("groups", "orb"), None),
        P(("groups", "orb"), None),
        P(("groups", "orb")),
    )
    out_specs = P(("groups", "orb"), None)
    return jax.shard_map(
        on_device, mesh=mesh, in_specs=in_specs, out_specs=out_specs, check_vma=False
    )
```
